256 devices in a mesh: seq: 8 (over x_lo, y), dp: 32 (over x_hi, z, core).
Axes of the slice: x: 4 (x_hi: 2, x_lo: 2; x = x_hi * 2 + x_lo), y: 4, z: 8, core: 2. Of those that a mesh axis runs over, the one named last changes fastest.
Arguments:
- tokens: bfloat16 [32768, 1536], P(('dp', 'seq')), parts along dimension 0, may hold values from -6 to 6
- dilations: int32 [2], replicated, may hold values from 1 to 128, as said below
- taps: float32 [2, 3, 1536], replicated, may hold values from -3 to 3
- w_query: bfloat16 [1536, 512], replicated, may hold values from -0.15625 to 0.15625
- w_keyval: bfloat16 [1536, 256], replicated, may hold values from -0.15625 to 0.15625
- w_out: bfloat16 [512, 1536], replicated, may hold values from -0.25 to 0.25
- exponents: int32 [256], P(('dp', 'seq')), parts along dimension 0, may hold values from -9 to -6
- pair: bfloat16 [2048, 64, 128], P(('dp', 'seq')), parts along dimension 0
- w_bias: float32 [128, 4], replicated
- cotangent: bfloat16 [32768, 1536], P(('dp', 'seq')), parts along dimension 0, may hold values from -6 to 6
Outputs:
- output: bfloat16 [32768, 1536], P(('dp', 'seq')), parts along dimension 0
- grad_tokens: bfloat16 [32768, 1536], P(('dp', 'seq')), parts along dimension 0
- grad_query: bfloat16 [49152, 512], P(('dp', 'seq')), parts along dimension 0
- grad_keyval: bfloat16 [49152, 256], P(('dp', 'seq')), parts along dimension 0
- grad_out: bfloat16 [16384, 1536], P(('dp', 'seq')), parts along dimension 0
The draws below stay inside these ranges and needn't reach their ends.
There are 32 independent parts, one for each index of `dp`. The reference program is written for one: setup_inputs(seed, part) draws one part's arguments, and reference() takes and returns one part's arrays. A program takes and returns all parts, laid end to end along the dimension named above; an argument that names none is the same for every part. Nothing has to cross between parts.
Inputs may be any that keep to these rules, and one draw needn't show every extreme that they name: One of the dilations equals 128.
All inputs are finite; a program needn't handle non-finite values.
Results may differ from the reference program's by a relative error of at most 0.025.
The reference program's roundings to bfloat16 on the way count: a program that leaves them out, or rounds other values in their place, can miss the bound.
Values may be sent and summed in bfloat16 or wider, within the bound.
No kernel may reach another device: no remote copies, remote signals or barrier semaphores. Data moves between devices by JAX's collectives and lax.ppermute only.
A program may use at most 64 MiB of HBM per device.

```python
import jax
import jax.numpy as jnp
from jax import lax

WIDTH = 1536
HEADS = 4
HEAD_DIM = 128
PAIR_CH = 128
ROWS = 128
LAYERS = 2
POOL = 16
BLOCK = 128
LENGTH = 1024
PAIRS = 64
KBLOCKS = 8
N_SEQ = 8


def draw_dilations(key, part):
    key = jax.random.fold_in(key, 5)
    left_key, right_key = jax.random.split(key)
    layer_values = jax.random.randint(left_key, (LAYERS,), 1, ROWS + 1)
    layer_values = layer_values.at[0].set(ROWS)
    shuffle = jax.random.permutation(right_key, LAYERS)
    return layer_values[shuffle].astype(jnp.int32)


def draw_pair(key, part):
    key = jax.random.fold_in(key, 11)
    keys_all = jax.random.split(key, 1)
    cells = jax.random.normal(keys_all[0], (PAIRS, PAIRS, PAIR_CH), jnp.float32)
    return cells.astype(jnp.bfloat16)


def draw_w_bias(key, part):
    key = jax.random.fold_in(key, 7)
    mapped = 0.06 * jax.random.normal(key, (PAIR_CH, HEADS), jnp.float32)
    return mapped


def with_ends(drawn, rng, low, high):
    longest = drawn.shape.index(max(drawn.shape))
    spots = []
    for shift in (0, 1):
        where = [jax.random.randint(jax.random.fold_in(rng, axis), (), 0, length) for axis, length in enumerate(drawn.shape)]
        where[longest] = (where[longest] + shift) % drawn.shape[longest]
        spots.append(tuple(where))
    return drawn.at[spots[0]].set(low).at[spots[1]].set(high)


def block_scale(key, extent, cuts, smallest, high):
    gain = 1.0
    for axis_at, parts in cuts:
        steps = jax.random.uniform(jax.random.fold_in(jax.random.fold_in(key, 6), axis_at), (parts,), jnp.float32, smallest / len(cuts), high / len(cuts))
        gain = gain * jnp.repeat(jnp.exp(steps), extent[axis_at] // parts).reshape((-1,) + (1,) * (len(extent) - 1 - axis_at))
    return gain


def bell_draw(stream_key, shape, spread, bound, cuts=(), dtype=jnp.bfloat16):
    gain = block_scale(stream_key, shape, cuts, -0.22, 0.18) if cuts else 1.0
    array = jax.random.normal(stream_key, shape, jnp.float32) * spread * gain
    return jnp.minimum(jnp.maximum(array, -bound), bound).astype(dtype)


def setup_inputs(seed: int = 0, part: int = 0) -> dict:
    arg_keys = jax.random.split(jax.random.key(seed), 11)
    part_splits = jax.random.split(jax.random.fold_in(arg_keys[10], part), 11)
    return {
        "tokens": bell_draw(part_splits[0], (LENGTH, WIDTH), 1.0, 6.0, ((0, 8),)),
        "dilations": draw_dilations(jax.random.fold_in(arg_keys[10], 71), part),
        "taps": bell_draw(arg_keys[2], (LAYERS, 3, WIDTH), 0.5, 3.0, (), jnp.float32),
        "w_query": bell_draw(arg_keys[3], (WIDTH, HEADS * HEAD_DIM), WIDTH ** -0.5, 0.15625),
        "w_keyval": bell_draw(arg_keys[4], (WIDTH, 2 * HEAD_DIM), WIDTH ** -0.5, 0.15625),
        "w_out": bell_draw(arg_keys[5], (HEADS * HEAD_DIM, WIDTH), (HEADS * HEAD_DIM) ** -0.5, 0.25),
        "exponents": with_ends(jax.random.randint(part_splits[6], (KBLOCKS,), -9, -5), jax.random.fold_in(part_splits[6], 1), -9, (-5) - 1).astype(jnp.int32),
        "pair": draw_pair(jax.random.fold_in(jax.random.fold_in(arg_keys[10], part), 71), part),
        "w_bias": draw_w_bias(jax.random.fold_in(arg_keys[10], 71), part),
        "cotangent": bell_draw(part_splits[9], (LENGTH, WIDTH), 1.0, 6.0, ((0, 8),)),
    }


CLIP_LEVEL = 448.0


def shifted(values, offset):
    amount = values.shape[0]
    padded = jnp.pad(values, ((amount, amount), (0, 0)))
    return lax.dynamic_slice_in_dim(padded, (amount + offset).astype(jnp.int32), amount, 0)


def silu_slope(values):
    sigma = jax.nn.sigmoid(values)
    return sigma * (1.0 + values * (1.0 - sigma))


def rounded(values):
    return lax.optimization_barrier(values.astype(jnp.bfloat16)).astype(jnp.float32)


def device_sum(left, right):
    left_parts = left.reshape(N_SEQ, ROWS, left.shape[1])
    right_parts = right.reshape(N_SEQ, ROWS, right.shape[1])

    def one_range(operands):
        return rounded(jnp.dot(operands[0].T, operands[1], preferred_element_type=jnp.float32))

    partial_terms = lax.map(one_range, (left_parts, right_parts))
    return jnp.sum(partial_terms, axis=0).astype(jnp.bfloat16)


def reference(tokens, dilations, taps, w_query, w_keyval, w_out, exponents, pair, w_bias, cotangent):
    score_scale = HEAD_DIM ** -0.5
    current = tokens
    pre_acts = []
    for section in range(LAYERS):
        dilation = dilations[section]
        conv_in = current.astype(jnp.float32)
        mixed = taps[section, 0] * shifted(conv_in, -dilation) + taps[section, 1] * conv_in + taps[section, 2] * shifted(conv_in, dilation)
        pre_acts.append(mixed)
        current = (conv_in + jax.nn.silu(mixed)).astype(jnp.bfloat16)
    trunk = current
    keyval = jnp.dot(trunk, w_keyval, preferred_element_type=jnp.float32)
    factor = jnp.repeat(jnp.exp2(exponents.astype(jnp.float32)), BLOCK)[:, None]
    unscaled = keyval / factor
    codes = jnp.clip(unscaled, -CLIP_LEVEL, CLIP_LEVEL).astype(jnp.bfloat16)
    inside = (jnp.abs(unscaled) < CLIP_LEVEL).astype(jnp.float32)
    restored = (codes.astype(jnp.float32) * factor).astype(jnp.bfloat16)
    keys = restored[:, :HEAD_DIM]
    values = restored[:, HEAD_DIM:]
    queries = jnp.dot(trunk, w_query, preferred_element_type=jnp.float32).astype(jnp.bfloat16)
    pair_float = pair.astype(jnp.float32)
    mirrored = 0.5 * (pair_float + jnp.transpose(pair_float, (1, 0, 2)))
    bias = jnp.einsum("ijc,ch->hij", mirrored, w_bias, precision=lax.Precision.HIGHEST)
    grad_attn = jnp.dot(cotangent, w_out.T, preferred_element_type=jnp.float32).astype(jnp.bfloat16)
    query_heads = jnp.transpose(queries.reshape(LENGTH, HEADS, HEAD_DIM), (1, 0, 2))
    grad_heads = jnp.transpose(grad_attn.reshape(LENGTH, HEADS, HEAD_DIM), (1, 0, 2))

    def head_pass(operands):
        query_head, bias_head, grad_head = operands
        wide_bias = jnp.repeat(jnp.repeat(bias_head, POOL, 0), POOL, 1)
        scores = jnp.dot(query_head, keys.T, preferred_element_type=jnp.float32) * score_scale + wide_bias
        highest = jnp.max(scores, axis=1, keepdims=True)
        weights = jnp.exp(scores - highest)
        probs = weights / jnp.sum(weights, axis=1, keepdims=True)
        probs_b = probs.astype(jnp.bfloat16)
        attended_head = jnp.dot(probs_b, values, preferred_element_type=jnp.float32).astype(jnp.bfloat16)
        slope = jnp.dot(grad_head, values.T, preferred_element_type=jnp.float32)
        centred = probs * (slope - jnp.sum(probs * slope, axis=1, keepdims=True))
        centred_b = centred.astype(jnp.bfloat16)
        grad_q_head = jnp.dot(centred_b, keys, preferred_element_type=jnp.float32) * score_scale
        grad_k_head = jnp.dot(centred_b.T, query_head, preferred_element_type=jnp.float32)
        grad_v_head = jnp.dot(probs_b.T, grad_head, preferred_element_type=jnp.float32)
        return attended_head, grad_q_head, grad_k_head, grad_v_head

    attended_all, grad_q_all, grad_k_all, grad_v_all = lax.map(head_pass, (query_heads, bias, grad_heads))
    attended = jnp.transpose(attended_all, (1, 0, 2)).reshape(LENGTH, HEADS * HEAD_DIM)
    output = (trunk.astype(jnp.float32) + jnp.dot(attended, w_out, preferred_element_type=jnp.float32)).astype(jnp.bfloat16)
    grad_out = device_sum(attended, cotangent)
    grad_q = jnp.transpose(grad_q_all, (1, 0, 2)).reshape(LENGTH, HEADS * HEAD_DIM).astype(jnp.bfloat16)
    grad_kv_f = jnp.concatenate([jnp.sum(grad_k_all, axis=0) * score_scale, jnp.sum(grad_v_all, axis=0)], axis=1) * inside
    grad_kv = grad_kv_f.astype(jnp.bfloat16)
    joined = jnp.concatenate([grad_q, grad_kv], axis=1)
    grad_in = device_sum(trunk, joined)
    grad_query = grad_in[:, :HEADS * HEAD_DIM]
    grad_keyval = grad_in[:, HEADS * HEAD_DIM:]
    flow = cotangent.astype(jnp.float32) + jnp.dot(grad_q, w_query.T, preferred_element_type=jnp.float32) + jnp.dot(grad_kv, w_keyval.T, preferred_element_type=jnp.float32)
    for section in reversed(range(LAYERS)):
        dilation = dilations[section]
        pushed = rounded(flow * silu_slope(pre_acts[section]))
        flow = flow + taps[section, 0] * shifted(pushed, dilation) + taps[section, 1] * pushed + taps[section, 2] * shifted(pushed, -dilation)
    return output, flow.astype(jnp.bfloat16), grad_query, grad_keyval, grad_out
```

```python
import jax
import jax.numpy as jnp
from jax import lax
from jax.experimental import pallas as pl
from jax.experimental.pallas import tpu as pltpu
from jax.sharding import PartitionSpec as P

POOL = 16
CLIP_LEVEL = 448.0
F32 = jnp.float32
BF16 = jnp.bfloat16
MIB = 1 << 20
VMEM = pl.BlockSpec(memory_space=pltpu.VMEM)
SMEM = pl.BlockSpec(memory_space=pltpu.SMEM)


def nn(a, b):
    return jnp.dot(a, b, preferred_element_type=F32)


def nt(a, b):
    return lax.dot_general(a, b, (((1,), (1,)), ((), ())), preferred_element_type=F32)


def call(body, outs, name, flops=0, nbytes=0, scratch=(), limit=40):
    def run(*args):
        specs = [SMEM if a.dtype == jnp.int32 else VMEM for a in args]
        shapes = [jax.ShapeDtypeStruct(s, d) for s, d in outs]
        single = len(shapes) == 1
        return pl.pallas_call(
            body,
            out_shape=shapes[0] if single else shapes,
            in_specs=specs,
            out_specs=VMEM if single else [VMEM] * len(shapes),
            scratch_shapes=list(scratch),
            compiler_params=pltpu.CompilerParams(vmem_limit_bytes=limit * MIB),
            cost_estimate=pl.CostEstimate(flops=flops, bytes_accessed=nbytes, transcendentals=0),
            name=name,
        )(*args)

    return run


def exchange(x):
    return lax.all_to_all(x, "seq", split_axis=0, concat_axis=0, tiled=True)


def flip_body(tok_ref, cot_ref, out_ref):
    n, rows, _ = out_ref.shape
    half = rows // 2
    for r in range(n):
        cols = pl.ds(r * half, half)
        out_ref[r, :half, :] = tok_ref[:, r * half : (r + 1) * half].astype(F32).T.astype(BF16)
        out_ref[r, half:, :] = cot_ref[:, r * half : (r + 1) * half].astype(F32).T.astype(BF16)


def split3(x):
    hi = x.astype(BF16)
    rest = x - hi.astype(F32)
    mid = rest.astype(BF16)
    lo = (rest - mid.astype(F32)).astype(BF16)
    return hi, mid, lo


def early_body(cot_ref, wout_ref, pair_ref, wb_ref, ga_ref, send_ref, own_ref):
    ga_ref[...] = nt(cot_ref[...], wout_ref[...]).astype(BF16)
    lane = lax.broadcasted_iota(jnp.int32, (128, 128), 1)
    head = (lane % 32) // 8
    wide = jnp.zeros((128, 128), F32)
    for h in range(4):
        wide = jnp.where(head == h, wb_ref[:, h : h + 1], wide)
    pieces = split3(wide)
    cells = jnp.zeros((64, 128), F32)
    for j in range(8):
        pick = lane % 8 == j
        for piece in pieces:
            cells += nn(pair_ref[j], jnp.where(pick, piece.astype(F32), 0.0).astype(BF16))
    hi, mid, lo = split3(cells)
    group = lax.broadcasted_iota(jnp.int32, (64, 128), 1) // 32
    packed = jnp.where(
        group == 0,
        hi.astype(F32),
        jnp.where(group == 1, mid.astype(F32), jnp.where(group == 2, lo.astype(F32), 0.0)),
    ).reshape(8, 8, 128)
    send_ref[...] = jnp.concatenate([packed, jnp.zeros((8, 8, 128), F32)], axis=1).astype(BF16)
    turned = jnp.concatenate([cells, cells], axis=0).T
    own_ref[...] = turned[:32, :]


def sigmoid(v):
    return 1.0 / (1.0 + jnp.exp(-v))


def shifts(blocks, d):
    lane = lax.broadcasted_iota(jnp.int32, blocks[0].shape, 1)
    turn = lax.rem(d, 128)
    back = 128 - d
    rolled = [pltpu.roll(b, turn, 1) for b in blocks]
    other = [pltpu.roll(b, back, 1) for b in blocks]
    zero = jnp.zeros_like(blocks[0])
    count = len(blocks)
    before = [
        jnp.where(lane < d, rolled[s - 1] if s else zero, rolled[s]) for s in range(count)
    ]
    after = [
        jnp.where(lane >= back, other[s + 1] if s + 1 < count else zero, other[s])
        for s in range(count)
    ]
    return before, after


def conv_body(dil_ref, x_ref, taps_ref, cells_ref, out_ref, pre0_ref, pre1_ref):
    count = x_ref.shape[0]
    channels = pre0_ref.shape[1]

    def chunk(c, carry):
        rows = pl.ds(pl.multiple_of(c * 16, 16), 16)
        cur = [x_ref[s, rows, :].astype(F32) for s in range(count)]
        tap = taps_ref[rows, :]
        for layer, pre in ((0, pre0_ref), (1, pre1_ref)):
            t0, t1, t2 = (tap[:, 3 * layer + k : 3 * layer + k + 1] for k in range(3))
            before, after = shifts(cur, dil_ref[layer])
            for s in range(count):
                mixed = t0 * before[s] + t1 * cur[s] + t2 * after[s]
                pre[s, rows, :] = mixed
                cur[s] = (cur[s] + mixed * sigmoid(mixed)).astype(BF16).astype(F32)
        for s in range(count):
            out_ref[s, rows, :] = cur[s].astype(BF16)
        return carry

    lax.fori_loop(0, channels // 16, chunk, 0)
    out_ref[:, channels:, :] = cells_ref[...]


def power_of_two(e):
    up, down = F32(1.0), F32(1.0)
    size = jnp.abs(e)
    for bit in range(6):
        on = ((size >> bit) & 1) == 1
        up = up * jnp.where(on, F32(2.0 ** (1 << bit)), F32(1.0))
        down = down * jnp.where(on, F32(0.5 ** (1 << bit)), F32(1.0))
    return jnp.where(e >= 0, up, down), jnp.where(e >= 0, down, up)


def keyval_body(exp_ref, x_ref, wkv_ref, send_ref, inside_ref, trunk_ref):
    count, wide, _ = x_ref.shape
    channels = wide - 16
    for s in range(count):
        trunk_ref[:, s * channels : (s + 1) * channels] = (
            x_ref[s, :channels, :].astype(F32).T.astype(BF16)
        )
    factor, inverse = power_of_two(exp_ref[0])
    unscaled = nn(trunk_ref[...], wkv_ref[...]) * inverse
    codes = jnp.clip(unscaled, -CLIP_LEVEL, CLIP_LEVEL).astype(BF16)
    restored = (codes.astype(F32) * factor).astype(BF16)
    for s in range(count):
        send_ref[s] = restored
    inside_ref[...] = jnp.where(jnp.abs(unscaled) < CLIP_LEVEL, F32(1.0), F32(0.0)).T


def query_body(trunk_ref, wq_ref, x_ref, own_ref, q_ref, ext_ref):
    q_ref[...] = nn(trunk_ref[...], wq_ref[...]).astype(BF16)
    count, wide, _ = x_ref.shape
    row = lax.broadcasted_iota(jnp.int32, (128, 512), 0)
    col = lax.broadcasted_iota(jnp.int32, (128, 512), 1)
    same_head = (row % 32) // 8 == col // 128
    target = (row % 8) - (col % 64)
    mirrored = jnp.zeros((16, 512), F32)
    for s in range(count):
        pick = jnp.where(same_head & (row < 96) & (target == -8 * s), F32(1.0), F32(0.0))
        mirrored += nn(x_ref[s, wide - 16 :, :], pick.astype(BF16))
    lane = lax.broadcasted_iota(jnp.int32, (8, 128), 1)
    for h in range(4):
        bias = 0.5 * (own_ref[8 * h : 8 * h + 8, :] + mirrored[:8, 128 * h : 128 * h + 128])
        bias = bias * F32(128.0**0.5)
        hi = bias.astype(BF16).astype(F32)
        both = jnp.where(lane < 64, hi, bias - hi)
        wide_bias = jnp.broadcast_to(both[:, None, :], (8, POOL, 128)).reshape(128, 128)
        ext_ref[h] = wide_bias.astype(BF16)


def attention_body(q_ref, ext_ref, ga_ref, kv_ref, send_ref, bulk_ref, kx_ref, c_ref, p_ref):
    scale = F32(128.0**-0.5)
    count = kv_ref.shape[0]
    length = count * 128
    for s in range(count):
        kx_ref[s * 128 : (s + 1) * 128, :128] = kv_ref[s, :, :128]
    row = lax.broadcasted_iota(jnp.int32, (length, 128), 0)
    lane = lax.broadcasted_iota(jnp.int32, (length, 128), 1)
    kx_ref[:, 128:] = jnp.where(lane % 64 == row // POOL, F32(1.0), F32(0.0)).astype(BF16)
    keys = kx_ref[:, :128]
    values = kv_ref[:, :, 128:].reshape(length, 128)
    for h in range(4):
        cols = slice(128 * h, 128 * h + 128)
        query = q_ref[:, cols]
        grad = ga_ref[:, cols]
        scores = nt(jnp.concatenate([query, ext_ref[h]], axis=1), kx_ref[...]) * scale
        highest = jnp.max(scores, axis=1, keepdims=True)
        weights = jnp.exp(scores - highest)
        probs = weights * (1.0 / jnp.sum(weights, axis=1, keepdims=True))
        probs_b = probs.astype(BF16)
        p_ref[cols, :] = probs_b
        attended = nn(probs_b, values).astype(BF16)
        slope = nt(grad, values)
        mean = jnp.sum(probs * slope, axis=1, keepdims=True)
        centred_b = (probs * (slope - mean)).astype(BF16)
        c_ref[cols, :] = centred_b
        grad_q = (nn(centred_b, keys) * scale).astype(BF16)
        for s in range(count):
            bulk_ref[s, :, cols] = attended
            bulk_ref[s, :, 512 + 128 * h : 640 + 128 * h] = grad_q
    q_turned = jnp.concatenate(
        [q_ref[:, 128 * h : 128 * h + 128].astype(F32).T.astype(BF16) for h in range(4)], axis=1
    )
    g_turned = jnp.concatenate(
        [ga_ref[:, 128 * h : 128 * h + 128].astype(F32).T.astype(BF16) for h in range(4)], axis=1
    )
    grad_k = (nn(q_turned, c_ref[...]) * scale).astype(BF16)
    grad_v = nn(g_turned, p_ref[...]).astype(BF16)
    for s in range(count):
        send_ref[s, :128, :] = grad_k[:, s * 128 : (s + 1) * 128]
        send_ref[s, 128:, :] = grad_v[:, s * 128 : (s + 1) * 128]


def output_body(trunk_ref, bulk_ref, wout_ref, out_ref):
    out_ref[...] = (
        trunk_ref[...].astype(F32) + nn(bulk_ref[0, :, :512], wout_ref[...])
    ).astype(BF16)


def sum_body(x_ref, inside_ref, send_ref):
    count = x_ref.shape[0]
    total = x_ref[0].astype(F32)
    for s in range(1, count):
        total = total + x_ref[s].astype(F32)
    total = (total * inside_ref[...]).astype(BF16)
    for s in range(count):
        send_ref[s] = total


def back_body(
    dil_ref, bulk_ref, gkv_ref, x_ref, wq_ref, wkv_ref, taps_ref, pre0_ref, pre1_ref, out_ref, g_ref
):
    count = x_ref.shape[0]
    channels = x_ref.shape[1] // 2
    grad_out = jnp.zeros((channels, 512), F32)
    for s in range(count):
        turned = x_ref[s, channels:, :]
        g_ref[s] = (
            turned.astype(F32)
            + nt(wq_ref[...], bulk_ref[s, :, 512:])
            + nn(wkv_ref[...], gkv_ref[s])
        )
        grad_out += nn(turned, bulk_ref[s, :, :512])
    half = channels // 2
    for s in range(count):
        cols = grad_out[:, 64 * s : 64 * s + 64]
        out_ref[s, channels:, :] = jnp.concatenate([cols[:half], cols[half:]], axis=1).astype(BF16)

    def chunk(c, carry):
        rows = pl.ds(pl.multiple_of(c * 16, 16), 16)
        flow = [g_ref[s, rows, :] for s in range(count)]
        tap = taps_ref[rows, :]
        for layer, pre in ((1, pre1_ref), (0, pre0_ref)):
            t0, t1, t2 = (tap[:, 3 * layer + k : 3 * layer + k + 1] for k in range(3))
            pushed = []
            for s in range(count):
                v = pre[s, rows, :]
                sigma = sigmoid(v)
                slope = sigma * (1.0 + v * (1.0 - sigma))
                pushed.append((flow[s] * slope).astype(BF16).astype(F32))
            before, after = shifts(pushed, dil_ref[layer])
            flow = [
                flow[s] + t0 * after[s] + t1 * pushed[s] + t2 * before[s] for s in range(count)
            ]
        for s in range(count):
            out_ref[s, rows, :] = flow[s].astype(BF16)
        return carry

    lax.fori_loop(0, channels // 16, chunk, 0)


def weights_body(x_ref, bulk_ref, gkv_ref, gq_ref, gkv_out_ref):
    count = x_ref.shape[0]
    channels = gq_ref.shape[0]
    first = jnp.zeros(gq_ref.shape, F32)
    second = jnp.zeros(gkv_out_ref.shape, F32)
    for s in range(count):
        turned = x_ref[s, :channels, :]
        first += nn(turned, bulk_ref[s, :, 512:])
        second += nt(turned, gkv_ref[s])
    gq_ref[...] = first.astype(BF16)
    gkv_out_ref[...] = second.astype(BF16)


def last_body(x_ref, grad_ref, gout_ref):
    count = x_ref.shape[0]
    channels = 192
    half = channels // 2
    for s in range(count):
        grad_ref[:, s * channels : (s + 1) * channels] = (
            x_ref[s, :channels, :].astype(F32).T.astype(BF16)
        )
        turned = x_ref[s, channels:, :].astype(F32).T.astype(BF16)
        gout_ref[:, s * channels : s * channels + half] = turned[:64]
        gout_ref[:, s * channels + half : (s + 1) * channels] = turned[64:]


def local(tokens, dilations, taps, w_query, w_keyval, w_out, exponents, pair, w_bias, cotangent):
    count = lax.axis_size("seq")
    me = lax.axis_index("seq")
    rows, width = tokens.shape
    ch = width // count
    length = rows * count
    my_rows = me * ch
    my_taps = lax.dynamic_slice(taps.reshape(6, width), (0, my_rows), (6, ch)).T
    my_wq = lax.dynamic_slice(w_query, (my_rows, 0), (ch, 512))
    my_wkv = lax.dynamic_slice(w_keyval, (my_rows, 0), (ch, 256))

    first = call(flip_body, [((count, 2 * ch, rows), BF16)], "flip", 0, 4 * rows * width * 2)(
        tokens, cotangent
    )
    turned = exchange(first)
    grad_attn, cells, own = call(
        early_body,
        [((rows, 512), BF16), ((count, 16, 128), BF16), ((32, 128), F32)],
        "early",
        2 * rows * width * 512,
        4 * MIB,
    )(cotangent, w_out, pair, w_bias)

    trunk_cells, pre0, pre1 = call(
        conv_body,
        [
            ((count, ch + 16, rows), BF16),
            ((count, ch, rows), F32),
            ((count, ch, rows), F32),
        ],
        "conv",
        100 * length * ch,
        4 * MIB,
    )(dilations, turned, my_taps, cells)
    back = exchange(trunk_cells)

    restored, inside, trunk = call(
        keyval_body,
        [((count, rows, 256), BF16), ((256, rows), F32), ((rows, width), BF16)],
        "keyval",
        2 * rows * width * 256,
        2 * MIB,
    )(exponents, back, w_keyval)
    keyval = exchange(restored)
    queries, ext = call(
        query_body,
        [((rows, 512), BF16), ((4, rows, 128), BF16)],
        "query",
        2 * rows * width * 512,
        3 * MIB,
    )(trunk, w_query, back, own)

    partial, bulk = call(
        attention_body,
        [((count, 256, 128), BF16), ((count, rows, 1024), BF16)],
        "attention",
        12 * rows * length * 512,
        4 * MIB,
        scratch=[
            pltpu.VMEM((length, 256), BF16),
            pltpu.VMEM((512, length), BF16),
            pltpu.VMEM((512, length), BF16),
        ],
    )(queries, ext, grad_attn, keyval)
    partial = exchange(partial)
    bulk_all = exchange(bulk)
    output = call(output_body, [((rows, width), BF16)], "output", 2 * rows * width * 512, 3 * MIB)(
        trunk, bulk, w_out
    )
    grad_kv = call(sum_body, [((count, 256, 128), BF16)], "sum", 8 * 256 * 128, MIB)(
        partial, inside
    )
    gkv_all = exchange(grad_kv)

    final = call(
        back_body,
        [((count, ch + ch // 2, rows), BF16)],
        "back",
        2 * length * ch * 1280,
        8 * MIB,
        scratch=[pltpu.VMEM((count, ch, rows), F32)],
    )(dilations, bulk_all, gkv_all, turned, my_wq, my_wkv, my_taps, pre0, pre1)
    final = exchange(final)
    grad_query, grad_keyval = call(
        weights_body,
        [((ch, 512), BF16), ((ch, 256), BF16)],
        "weights",
        2 * length * ch * 768,
        4 * MIB,
    )(trunk_cells, bulk_all, gkv_all)
    grad_tokens, grad_out = call(
        last_body, [((rows, width), BF16), ((64, width), BF16)], "last", 0, 2 * MIB
    )(final)
    return output, grad_tokens, grad_query, grad_keyval, grad_out


def solution(mesh):
    both = P(("dp", "seq"))
    in_specs = (both, P(), P(), P(), P(), P(), both, both, P(), both)
    return jax.shard_map(
        local, mesh=mesh, in_specs=in_specs, out_specs=(both,) * 5, check_vma=False
    )
```

```python
import jax
import jax.numpy as jnp
from jax import lax
from jax.experimental import pallas as pl
from jax.experimental.pallas import tpu as pltpu
from jax.sharding import PartitionSpec as P

POOL = 16
CLIP_LEVEL = 448.0
F32 = jnp.float32
BF16 = jnp.bfloat16
MIB = 1 << 20
VMEM = pl.BlockSpec(memory_space=pltpu.VMEM)
SMEM = pl.BlockSpec(memory_space=pltpu.SMEM)


def nn(a, b):
    return jnp.dot(a, b, preferred_element_type=F32)


def nt(a, b):
    return lax.dot_general(a, b, (((1,), (1,)), ((), ())), preferred_element_type=F32)


def call(body, outs, name, flops=0, nbytes=0, scratch=(), limit=16):
    def run(*args):
        return pl.pallas_call(
            body,
            out_shape=[jax.ShapeDtypeStruct(s, d) for s, d in outs],
            in_specs=[SMEM if a.dtype == jnp.int32 else VMEM for a in args],
            out_specs=[VMEM] * len(outs),
            scratch_shapes=list(scratch),
            compiler_params=pltpu.CompilerParams(vmem_limit_bytes=limit * MIB),
            cost_estimate=pl.CostEstimate(flops=flops, bytes_accessed=nbytes, transcendentals=0),
            name=name,
        )(*args)

    return run


def exchange(x):
    return lax.all_to_all(x, "seq", split_axis=0, concat_axis=0, tiled=True)


def after(x, *others):
    return lax.optimization_barrier((x, *others))[0]


def flip_body(tok_ref, cot_ref, out_ref):
    n, rows, _ = out_ref.shape
    half = rows // 2
    for r in range(n):
        cols = slice(r * half, (r + 1) * half)
        out_ref[r, :half, :] = tok_ref[:, cols].astype(F32).T.astype(BF16)
        out_ref[r, half:, :] = cot_ref[:, cols].astype(F32).T.astype(BF16)


def split3(x):
    hi = x.astype(BF16)
    rest = x - hi.astype(F32)
    mid = rest.astype(BF16)
    lo = (rest - mid.astype(F32)).astype(BF16)
    return hi, mid, lo


def early_body(
    exp_ref, me_ref, cot_ref, wout_ref, pair_ref, wb_ref, taps_ref, out_ref, my_taps_ref, turn_ref
):
    ch = my_taps_ref.shape[0]
    begin = me_ref[0] * ch
    window = begin // 128 * 128
    for layer in range(2):
        part = taps_ref[layer, :, pl.ds(pl.multiple_of(window, 128), 256)]
        for k in range(3):
            turn_ref[:, 8 * layer + k : 8 * layer + k + 1] = part[k : k + 1, :].T
    my_taps_ref[...] = turn_ref[pl.ds(pl.multiple_of(begin - window, 8), ch), :]
    lane = lax.broadcasted_iota(jnp.int32, (128, 128), 1)
    head = (lane % 32) // 8
    wide = jnp.zeros((128, 128), F32)
    for h in range(4):
        wide = jnp.where(head == h, wb_ref[:, h : h + 1], wide)
    pieces = split3(wide)
    cells = jnp.zeros((64, 128), F32)
    for j in range(8):
        pick = lane % 8 == j
        for piece in pieces:
            cells += nn(pair_ref[j], jnp.where(pick, piece.astype(F32), 0.0).astype(BF16))
    hi, mid, lo = (piece.astype(F32) for piece in split3(cells))
    group = lax.broadcasted_iota(jnp.int32, (64, 128), 1) // 32
    factor, _ = power_of_two(exp_ref[0])
    packed = jnp.where(group == 0, hi, jnp.where(group == 1, mid, jnp.where(group == 2, lo, factor)))
    out_ref[512:, :] = packed.astype(BF16)
    grad = nt(cot_ref[...], wout_ref[...]).astype(BF16)
    for h in range(4):
        out_ref[128 * h : 128 * h + 128, :] = grad[:, 128 * h : 128 * h + 128]


def sigmoid(v):
    return 0.5 * jnp.tanh(0.5 * v) + 0.5


def shifts(blocks, d):
    lane = lax.broadcasted_iota(jnp.int32, blocks[0].shape, 1)
    turn = lax.rem(d, 128)
    back = 128 - d
    rolled = [pltpu.roll(b, turn, 1) for b in blocks]
    other = [pltpu.roll(b, back, 1) for b in blocks]
    zero = jnp.zeros_like(blocks[0])
    count = len(blocks)
    before = [
        jnp.where(lane < d, rolled[s - 1] if s else zero, rolled[s]) for s in range(count)
    ]
    after = [
        jnp.where(lane >= back, other[s + 1] if s + 1 < count else zero, other[s])
        for s in range(count)
    ]
    return before, after


def conv_body(dil_ref, x_ref, taps_ref, out_ref, slope_ref):
    count, channels, _ = out_ref.shape

    def chunk(c, carry):
        rows = pl.ds(pl.multiple_of(c * 16, 16), 16)
        cur = [x_ref[s, rows, :].astype(F32) for s in range(count)]
        tap = taps_ref[rows, :]
        for layer in range(2):
            t0, t1, t2 = (tap[:, 8 * layer + k : 8 * layer + k + 1] for k in range(3))
            before, after = shifts(cur, dil_ref[layer])
            for s in range(count):
                mixed = t0 * before[s] + t1 * cur[s] + t2 * after[s]
                sigma = sigmoid(mixed)
                gated = mixed * sigma
                slope_ref[layer, s, rows, :] = (sigma + gated * (1.0 - sigma)).astype(BF16)
                cur[s] = (cur[s] + gated).astype(BF16).astype(F32)
        for s in range(count):
            out_ref[s, rows, :] = cur[s].astype(BF16)
        return carry

    lax.fori_loop(0, channels // 16, chunk, 0)


def power_of_two(e):
    up, down = F32(1.0), F32(1.0)
    size = jnp.abs(e)
    for bit in range(6):
        on = ((size >> bit) & 1) == 1
        up = up * jnp.where(on, F32(2.0 ** (1 << bit)), F32(1.0))
        down = down * jnp.where(on, F32(0.5 ** (1 << bit)), F32(1.0))
    return jnp.where(e >= 0, up, down), jnp.where(e >= 0, down, up)


def keyval_body(exp_ref, x_ref, wkv_ref, wq_ref, send_ref, trunk_ref):
    count, channels, _ = x_ref.shape
    for s in range(count):
        trunk_ref[:, s * channels : (s + 1) * channels] = x_ref[s].astype(F32).T.astype(BF16)
    factor, inverse = power_of_two(exp_ref[0])
    unscaled = nn(trunk_ref[...], wkv_ref[...]) * inverse
    codes = jnp.clip(unscaled, -CLIP_LEVEL, CLIP_LEVEL).astype(BF16).astype(F32)
    marked = jnp.where(
        jnp.abs(unscaled) < CLIP_LEVEL, codes, jnp.where(unscaled > 0.0, F32(512.0), F32(-512.0))
    )
    marked = (marked * factor).astype(BF16)
    query = nn(trunk_ref[...], wq_ref[...]).astype(BF16)
    for s in range(count):
        send_ref[s, :, :256] = marked
        send_ref[s, :, 256:] = query


def query_body(me_ref, *refs):
    columns, (pack_ref, cells_ref) = refs[:8], refs[8:]
    me = me_ref[0]
    x, y = me // 4, lax.rem(me, 4)
    count = cells_ref.shape[0]
    for k, ref in enumerate(columns):
        block = (x if k < 4 else 1 - x) * 4 + lax.rem(y + (0, 3, 1, 2)[k % 4], 4)
        cells_ref[block] = ref[512:, :]
        pack_ref[block, :512, :] = ref[:512, :]
    row = lax.broadcasted_iota(jnp.int32, (128, 512), 0)
    col = lax.broadcasted_iota(jnp.int32, (128, 512), 1)
    same_head = (row % 32) // 8 == col // 128
    target = (row % 8) - (col % 64)
    mirrored = jnp.zeros((64, 512), F32)
    for s in range(count):
        pick = jnp.where(same_head & (row < 96) & (target == -8 * s), F32(1.0), F32(0.0))
        mirrored += nn(cells_ref[s], pick.astype(BF16))
    lane = lax.broadcasted_iota(jnp.int32, (64, 128), 1)
    for h in range(4):
        one = mirrored[:, 128 * h : 128 * h + 128]
        other = jnp.concatenate([one, one], axis=0).T
        bias = 0.5 * (one + other[:64, :]) * F32(128.0**0.5)
        hi = bias.astype(BF16).astype(F32)
        both = jnp.where(lane < 64, hi, bias - hi).astype(BF16)
        for s in range(count):
            wide = both[8 * s : 8 * s + 8].astype(F32)
            wide = jnp.broadcast_to(wide[:, None, :], (8, POOL, 128)).reshape(128, 128)
            pack_ref[s, 512 + 128 * h : 640 + 128 * h, :] = wide.astype(BF16)
    for s in range(count):
        corner = cells_ref[s, 0:1, 127:128].astype(F32)
        pack_ref[s, 1024:, :] = jnp.broadcast_to(corner, (16, 128)).astype(BF16)


def attention_body(
    kv_ref, pack_ref, att_ref, gq_ref, out_ref,
    sum_ref, kx_ref, v_ref, kt_ref, vt_ref, qx_ref, s_ref, sl_ref, pb_ref, cb_ref,
):
    scale = F32(128.0**-0.5)
    count = kv_ref.shape[0]
    length = count * 128
    for s in range(count):
        rows = slice(128 * s, 128 * s + 128)
        level = pack_ref[s, 1024:1025, 0:1].astype(F32) * CLIP_LEVEL
        plain = jnp.clip(kv_ref[s, :, :256].astype(F32), -level, level)
        kx_ref[rows, :128] = plain[:, :128].astype(BF16)
        v_ref[rows, :] = plain[:, 128:].astype(BF16)
        kt_ref[:, rows] = plain[:, :128].T.astype(BF16)
        vt_ref[:, rows] = plain[:, 128:].T.astype(BF16)
        for h in range(4):
            here = slice(128 * h, 128 * h + 128)
            qx_ref[s, here, :128] = kv_ref[s, :, 256 + 128 * h : 384 + 128 * h]
            qx_ref[s, here, 128:] = pack_ref[s, 512 + 128 * h : 640 + 128 * h, :]
    row = lax.broadcasted_iota(jnp.int32, (length, 128), 0)
    lane = lax.broadcasted_iota(jnp.int32, (length, 128), 1)
    kx_ref[:, 128:] = jnp.where(lane % 64 == row // POOL, F32(1.0), F32(0.0)).astype(BF16)
    sum_ref[...] = jnp.zeros_like(sum_ref)

    size = 256
    pieces = [slice(c * size, (c + 1) * size) for c in range(length // size)]
    fold = (size // 8, 8, 512)

    def step(i, carry):
        query_x = qx_ref[i]
        query = query_x[:, :128]
        grad = pack_ref[i, :512, :]
        top = None
        for r in pieces:
            part = nt(kx_ref[r, :], query_x)
            s_ref[r, :] = part
            part = jnp.max(part.reshape(fold), axis=0)
            top = part if top is None else jnp.maximum(top, part)
        top = jnp.max(top, axis=0, keepdims=True)
        total = mean = jnp.zeros((8, 512), F32)
        for r in pieces:
            weights = jnp.exp2((s_ref[r, :] - top) * (scale * F32(1.4426950408889634)))
            slope = nt(v_ref[r, :], grad)
            s_ref[r, :] = weights
            sl_ref[r, :] = slope
            total += jnp.sum(weights.reshape(fold), axis=0)
            mean += jnp.sum((weights * slope).reshape(fold), axis=0)
        inverse = 1.0 / jnp.sum(total, axis=0, keepdims=True)
        mean = jnp.sum(mean, axis=0, keepdims=True) * inverse
        for r in pieces:
            probs = s_ref[r, :] * inverse
            probs_b = probs.astype(BF16)
            centred_b = (probs * (sl_ref[r, :] - mean)).astype(BF16)
            pb_ref[r, :] = probs_b
            cb_ref[r, :] = centred_b
            sum_ref[r, :128] += nn(centred_b, query)
            sum_ref[r, 128:] += nn(probs_b, grad)
        attended = nn(vt_ref[...], pb_ref[...]).astype(BF16)
        grad_q = (nn(kt_ref[...], cb_ref[...]) * scale).astype(BF16)
        for h in range(4):
            here = slice(128 * h, 128 * h + 128)
            att_ref[i, here, :] = attended[:, here]
            gq_ref[i, here, :] = grad_q[:, here]
        return carry

    lax.fori_loop(0, count, step, 0)
    side = lax.broadcasted_iota(jnp.int32, (128, 256), 1)
    for s in range(count):
        level = pack_ref[s, 1024:1025, 0:1].astype(F32) * CLIP_LEVEL
        inside = jnp.abs(kv_ref[s, :, :256].astype(F32)) <= level
        part = sum_ref[128 * s : 128 * s + 128, :]
        part = jnp.where(side < 128, part * scale, part)
        out_ref[s] = jnp.where(inside, part, 0.0).astype(BF16)


def output_body(me_ref, trunk_ref, att_ref, wout_ref, out_ref):
    me = me_ref[0]
    total = trunk_ref[...].astype(F32)
    for h in range(4):
        here = slice(128 * h, 128 * h + 128)
        total += nn(att_ref[me, here, :].astype(F32).T.astype(BF16), wout_ref[here, :])
    out_ref[...] = total.astype(BF16)


def back_body(
    dil_ref, me_ref, x_ref, att_ref, gq_ref, gkv_ref, wq_ref, wkv_ref, taps_ref, slope_ref,
    out_ref, g_ref,
):
    count, channels, _ = g_ref.shape
    mine = pl.ds(pl.multiple_of(me_ref[0] * channels, 16), channels)
    my_wq, my_wkv = wq_ref[mine, :], wkv_ref[mine, :]
    grad_out = jnp.zeros((channels, 512), F32)
    for s in range(count):
        turned = x_ref[s, channels:, :]
        g_ref[s] = turned.astype(F32) + nn(my_wq, gq_ref[s]) + nt(my_wkv, gkv_ref[s])
        grad_out += nt(turned, att_ref[s])
    half = channels // 2
    for s in range(count):
        cols = grad_out[:, 64 * s : 64 * s + 64]
        out_ref[s, channels:, :] = jnp.concatenate([cols[:half], cols[half:]], axis=1).astype(BF16)

    def chunk(c, carry):
        rows = pl.ds(pl.multiple_of(c * 16, 16), 16)
        flow = [g_ref[s, rows, :] for s in range(count)]
        tap = taps_ref[rows, :]
        for layer in (1, 0):
            t0, t1, t2 = (tap[:, 8 * layer + k : 8 * layer + k + 1] for k in range(3))
            pushed = [
                (flow[s] * slope_ref[layer, s, rows, :].astype(F32)).astype(BF16).astype(F32)
                for s in range(count)
            ]
            before, after = shifts(pushed, dil_ref[layer])
            flow = [
                flow[s] + t0 * after[s] + t1 * pushed[s] + t2 * before[s] for s in range(count)
            ]
        for s in range(count):
            out_ref[s, rows, :] = flow[s].astype(BF16)
        return carry

    lax.fori_loop(0, channels // 16, chunk, 0)


def weights_body(x_ref, gq_ref, gkv_ref, gq_out_ref, gkv_out_ref):
    count, channels, _ = x_ref.shape
    first = jnp.zeros(gq_out_ref.shape, F32)
    second = jnp.zeros(gkv_out_ref.shape, F32)
    for s in range(count):
        first += nt(x_ref[s], gq_ref[s])
        second += nn(x_ref[s], gkv_ref[s])
    gq_out_ref[...] = first.astype(BF16)
    gkv_out_ref[...] = second.astype(BF16)


def last_body(x_ref, grad_ref, gout_ref):
    count, wide, _ = x_ref.shape
    channels = grad_ref.shape[1] // count
    half = wide - channels
    for s in range(count):
        grad_ref[:, s * channels : (s + 1) * channels] = (
            x_ref[s, :channels, :].astype(F32).T.astype(BF16)
        )
        turned = x_ref[s, channels:, :].astype(F32).T.astype(BF16)
        gout_ref[:, s * channels : s * channels + half] = turned[:64]
        gout_ref[:, s * channels + half : (s + 1) * channels] = turned[64:]


def local(tokens, dilations, taps, w_query, w_keyval, w_out, exponents, pair, w_bias, cotangent):
    count = lax.axis_size("seq")
    me = lax.axis_index("seq")
    rows, width = tokens.shape
    ch = width // count
    length = rows * count
    place = me.astype(jnp.int32).reshape(1)
    blocks = (count, ch, rows)

    (first,) = call(flip_body, [((count, 2 * ch, rows), BF16)], "flip", 0, 4 * rows * width, limit=63)(
        tokens, cotangent
    )
    turned = exchange(first)
    grad_attn, my_taps = call(
        early_body,
        [((576, 128), BF16), ((ch, 16), F32)],
        "early",
        2 * rows * width * 512,
        4 * MIB,
        scratch=[pltpu.VMEM((256, 16), F32)],
    )(exponents, place, cotangent, w_out, pair, w_bias, taps)
    across = [(i, (i + 4) % 8) for i in range(8)]
    columns = [grad_attn] + [
        lax.ppermute(grad_attn, "seq", [(i, i // 4 * 4 + (i + o) % 4) for i in range(8)])
        for o in (1, 3, 2)
    ]
    other = [lax.ppermute(grad_attn, "seq", across)]

    trunk_turned, slopes = call(
        conv_body,
        [(blocks, BF16), ((2, *blocks), BF16)],
        "conv",
        100 * length * ch,
        4 * MIB,
    )(dilations, after(turned, grad_attn, my_taps), my_taps)
    back = exchange(after(trunk_turned, *columns, *other))
    other += [lax.ppermute(c, "seq", across) for c in columns[1:]]

    keyval, trunk = call(
        keyval_body,
        [((count, rows, 768), BF16), ((rows, width), BF16)],
        "keyval",
        2 * rows * width * 768,
        2 * MIB,
    )(exponents, back, w_keyval, w_query)
    keyval = exchange(after(keyval, *other))
    columns = columns + other
    (pack,) = call(
        query_body,
        [((count, 1040, 128), BF16)],
        "query",
        2 * rows * width * 512,
        3 * MIB,
        scratch=[pltpu.VMEM((count, 64, 128), BF16)],
    )(place, *columns)

    heads = (count, 512, 128)
    attended, grad_q, grad_kv = call(
        attention_body,
        [(heads, BF16), (heads, BF16), ((count, rows, 256), BF16)],
        "attention",
        12 * length * length * 512,
        8 * MIB,
        scratch=[
            pltpu.VMEM((length, 256), F32),
            pltpu.VMEM((length, 256), BF16),
            pltpu.VMEM((length, 128), BF16),
            pltpu.VMEM((128, length), BF16),
            pltpu.VMEM((128, length), BF16),
            pltpu.VMEM((count, 512, 256), BF16),
            pltpu.VMEM((length, 512), F32),
            pltpu.VMEM((length, 512), F32),
            pltpu.VMEM((length, 512), BF16),
            pltpu.VMEM((length, 512), BF16),
        ],
        limit=24,
    )(keyval, pack)

    (final,) = call(
        back_body,
        [((count, ch + ch // 2, rows), BF16)],
        "back",
        2 * length * ch * 1280,
        8 * MIB,
        scratch=[pltpu.VMEM(blocks, F32)],
    )(dilations, place, turned, attended, grad_q, grad_kv, w_query, w_keyval, my_taps, slopes)
    final = exchange(final)
    grad_query, grad_keyval = call(
        weights_body,
        [((ch, 512), BF16), ((ch, 256), BF16)],
        "weights",
        2 * length * ch * 768,
        4 * MIB,
    )(trunk_turned, grad_q, grad_kv)
    (output,) = call(output_body, [((rows, width), BF16)], "output", 2 * rows * width * 512, 3 * MIB)(
        place, trunk, attended, w_out
    )
    grad_tokens, grad_out = call(
        last_body, [((rows, width), BF16), ((64, width), BF16)], "last", 0, 2 * MIB
    )(final)
    return output, grad_tokens, grad_query, grad_keyval, grad_out


def solution(mesh):
    both = P(("dp", "seq"))
    in_specs = (both, P(), P(), P(), P(), P(), both, both, P(), both)
    return jax.shard_map(
        local, mesh=mesh, in_specs=in_specs, out_specs=(both,) * 5, check_vma=False
    )
```

```python
import jax
import jax.numpy as jnp
from jax import lax
from jax.experimental import pallas as pl
from jax.experimental.pallas import tpu as pltpu
from jax.sharding import PartitionSpec as P

POOL = 16
CLIP_LEVEL = 448.0
RUN = 4
CONV_LIMIT = 16
F32 = jnp.float32
BF16 = jnp.bfloat16
MIB = 1 << 20
VMEM = pl.BlockSpec(memory_space=pltpu.VMEM)
SMEM = pl.BlockSpec(memory_space=pltpu.SMEM)
ANY = pl.BlockSpec(memory_space=pl.ANY)


def nn(a, b):
    return jnp.dot(a, b, preferred_element_type=F32)


def nt(a, b):
    return lax.dot_general(a, b, (((1,), (1,)), ((), ())), preferred_element_type=F32)


def call(body, outs, name, flops=0, nbytes=0, scratch=(), limit=16, space=VMEM):
    def run(*args):
        return pl.pallas_call(
            body,
            out_shape=[jax.ShapeDtypeStruct(s, d) for s, d in outs],
            in_specs=[SMEM if a.dtype == jnp.int32 else space for a in args],
            out_specs=[space] * len(outs),
            scratch_shapes=list(scratch),
            compiler_params=pltpu.CompilerParams(vmem_limit_bytes=limit * MIB),
            cost_estimate=pl.CostEstimate(flops=flops, bytes_accessed=nbytes, transcendentals=0),
            name=name,
        )(*args)

    return run


def exchange(x):
    return lax.all_to_all(x, "seq", split_axis=0, concat_axis=0, tiled=True)


def after(x, *others):
    return lax.optimization_barrier((x, *others))[0]


def flip_body(tok_hbm, cot_hbm, out_hbm, tok_ref, cot_ref, out_ref, sems):
    n, rows, _ = out_ref.shape
    half = rows // 2
    reads = [
        pltpu.make_async_copy(tok_hbm, tok_ref, sems.at[n]),
        pltpu.make_async_copy(cot_hbm, cot_ref, sems.at[n + 1]),
    ]
    for copy in reads:
        copy.start()
    reads[0].wait()
    for r in range(n):
        out_ref[r, :half, :] = tok_ref[:, r * half : (r + 1) * half].astype(F32).T.astype(BF16)
    reads[1].wait()
    writes = []
    for r in range(n):
        out_ref[r, half:, :] = cot_ref[:, r * half : (r + 1) * half].astype(F32).T.astype(BF16)
        writes.append(pltpu.make_async_copy(out_ref.at[r], out_hbm.at[r], sems.at[r]))
        writes[r].start()
    for copy in writes:
        copy.wait()


def split3(x):
    hi = x.astype(BF16)
    rest = x - hi.astype(F32)
    mid = rest.astype(BF16)
    lo = (rest - mid.astype(F32)).astype(BF16)
    return hi, mid, lo


def take_taps(me, taps_ref, turn_ref):
    begin = me * 192
    window = begin // 128 * 128
    for k in range(3):
        part = taps_ref[k, :, pl.ds(pl.multiple_of(window, 128), 256)]
        for layer in range(2):
            turn_ref[:, 8 * layer + k : 8 * layer + k + 1] = part[layer : layer + 1, :].T
    return begin - window


def early_body(exp_ref, cot_ref, wout_ref, pair_ref, wb_ref, out_ref):
    weights = jnp.concatenate([wb_ref[...], wb_ref[...]], axis=0).T
    lane = lax.broadcasted_iota(jnp.int32, (128, 128), 1)
    head = (lane % 32) // 8
    wide = jnp.zeros((128, 128), F32)
    for h in range(4):
        wide = jnp.where(head == h, weights[:, h : h + 1], wide)
    pieces = split3(wide)
    cells = jnp.zeros((64, 128), F32)
    for j in range(8):
        pick = lane % 8 == j
        for piece in pieces:
            cells += nn(pair_ref[j], jnp.where(pick, piece.astype(F32), 0.0).astype(BF16))
    hi, mid, lo = (piece.astype(F32) for piece in split3(cells))
    group = lax.broadcasted_iota(jnp.int32, (64, 128), 1) // 32
    factor, _ = power_of_two(exp_ref[0])
    packed = jnp.where(group == 0, hi, jnp.where(group == 1, mid, jnp.where(group == 2, lo, factor)))
    out_ref[512:, :] = packed.astype(BF16)
    grad = nt(cot_ref[...], wout_ref[...]).astype(BF16)
    for h in range(4):
        out_ref[128 * h : 128 * h + 128, :] = grad[:, 128 * h : 128 * h + 128]


def sigmoid(v):
    return 0.5 * jnp.tanh(0.5 * v) + 0.5


def shifts(blocks, d):
    lane = lax.broadcasted_iota(jnp.int32, blocks[0].shape, 1)
    turn = lax.rem(d, 128)
    back = 128 - d
    rolled = [pltpu.roll(b, turn, 1) for b in blocks]
    other = [pltpu.roll(b, back, 1) for b in blocks]
    zero = jnp.zeros_like(blocks[0])
    count = len(blocks)
    before = [
        jnp.where(lane < d, rolled[s - 1] if s else zero, rolled[s]) for s in range(count)
    ]
    after = [
        jnp.where(lane >= back, other[s + 1] if s + 1 < count else zero, other[s])
        for s in range(count)
    ]
    return before, after


def conv_body(dil_ref, me_ref, x_ref, taps_ref, out_ref, slope_ref, turn_ref):
    offset = take_taps(me_ref[0], taps_ref, turn_ref)
    count, channels, _ = out_ref.shape

    def chunk(c, carry):
        rows = pl.ds(pl.multiple_of(c * 16, 16), 16)
        cur = [x_ref[s, rows, :].astype(F32) for s in range(count)]
        tap = turn_ref[pl.ds(pl.multiple_of(offset + c * 16, 16), 16), :]
        for layer in range(2):
            t0, t1, t2 = (tap[:, 8 * layer + k : 8 * layer + k + 1] for k in range(3))
            before, after = shifts(cur, dil_ref[layer])
            for s in range(count):
                mixed = t0 * before[s] + t1 * cur[s] + t2 * after[s]
                sigma = sigmoid(mixed)
                gated = mixed * sigma
                slope_ref[layer, s, rows, :] = (sigma + gated * (1.0 - sigma)).astype(BF16)
                cur[s] = (cur[s] + gated).astype(BF16).astype(F32)
        for s in range(count):
            out_ref[s, rows, :] = cur[s].astype(BF16)
        return carry

    lax.fori_loop(0, channels // 16, chunk, 0)


def power_of_two(e):
    up, down = F32(1.0), F32(1.0)
    size = jnp.abs(e)
    for bit in range(6):
        on = ((size >> bit) & 1) == 1
        up = up * jnp.where(on, F32(2.0 ** (1 << bit)), F32(1.0))
        down = down * jnp.where(on, F32(0.5 ** (1 << bit)), F32(1.0))
    return jnp.where(e >= 0, up, down), jnp.where(e >= 0, down, up)


def keyval_body(exp_ref, x_ref, wkv_ref, wq_ref, send_ref, trunk_ref):
    count, channels, _ = x_ref.shape
    for s in range(count):
        trunk_ref[:, s * channels : (s + 1) * channels] = x_ref[s].astype(F32).T.astype(BF16)
    factor, inverse = power_of_two(exp_ref[0])
    unscaled = nn(trunk_ref[...], wkv_ref[...]) * inverse
    codes = jnp.clip(unscaled, -CLIP_LEVEL, CLIP_LEVEL).astype(BF16).astype(F32)
    marked = jnp.where(
        jnp.abs(unscaled) < CLIP_LEVEL, codes, jnp.where(unscaled > 0.0, F32(512.0), F32(-512.0))
    )
    marked = (marked * factor).astype(BF16)
    query = nn(trunk_ref[...], wq_ref[...]).astype(BF16)
    for s in range(count):
        send_ref[s, :, :256] = marked
        send_ref[s, :, 256:] = query


def query_body(me_ref, *refs):
    columns, (pack_ref, cells_ref) = refs[:8], refs[8:]
    me = me_ref[0]
    x, y = me // 4, lax.rem(me, 4)
    count = cells_ref.shape[0]
    for k, ref in enumerate(columns):
        block = (x if k < 4 else 1 - x) * 4 + lax.rem(y + (0, 3, 1, 2)[k % 4], 4)
        cells_ref[block] = ref[512:, :]
        pack_ref[block, :512, :] = ref[:512, :]
    row = lax.broadcasted_iota(jnp.int32, (128, 512), 0)
    col = lax.broadcasted_iota(jnp.int32, (128, 512), 1)
    same_head = (row % 32) // 8 == col // 128
    target = (row % 8) - (col % 64)
    mirrored = jnp.zeros((64, 512), F32)
    for s in range(count):
        pick = jnp.where(same_head & (row < 96) & (target == -8 * s), F32(1.0), F32(0.0))
        mirrored += nn(cells_ref[s], pick.astype(BF16))
    lane = lax.broadcasted_iota(jnp.int32, (64, 128), 1)
    for h in range(4):
        one = mirrored[:, 128 * h : 128 * h + 128]
        other = jnp.concatenate([one, one], axis=0).T
        bias = 0.5 * (one + other[:64, :]) * F32(128.0**0.5)
        hi = bias.astype(BF16).astype(F32)
        both = jnp.where(lane < 64, hi, bias - hi).astype(BF16)
        for s in range(count):
            wide = both[8 * s : 8 * s + 8].astype(F32)
            wide = jnp.broadcast_to(wide[:, None, :], (8, POOL, 128)).reshape(128, 128)
            pack_ref[s, 512 + 128 * h : 640 + 128 * h, :] = wide.astype(BF16)
    for s in range(count):
        corner = cells_ref[s, 0:1, 127:128].astype(F32)
        pack_ref[s, 1024:, :] = jnp.broadcast_to(corner, (16, 128)).astype(BF16)


def attention_body(
    kv_ref, pack_ref, att_ref, gq_ref, out_ref,
    sum_ref, kx_ref, v_ref, kt_ref, vt_ref, qx_ref, s_ref, sl_ref, pb_ref, cb_ref,
):
    scale = F32(128.0**-0.5)
    count = kv_ref.shape[0]
    length = count * 128
    for s in range(count):
        rows = slice(128 * s, 128 * s + 128)
        level = pack_ref[s, 1024:1025, 0:1].astype(F32) * CLIP_LEVEL
        plain = jnp.clip(kv_ref[s, :, :256].astype(F32), -level, level)
        kx_ref[rows, :128] = plain[:, :128].astype(BF16)
        v_ref[rows, :] = plain[:, 128:].astype(BF16)
        kt_ref[:, rows] = plain[:, :128].T.astype(BF16)
        vt_ref[:, rows] = plain[:, 128:].T.astype(BF16)
        for h in range(4):
            here = slice(128 * h, 128 * h + 128)
            qx_ref[s, here, :128] = kv_ref[s, :, 256 + 128 * h : 384 + 128 * h]
            qx_ref[s, here, 128:] = pack_ref[s, 512 + 128 * h : 640 + 128 * h, :]
    row = lax.broadcasted_iota(jnp.int32, (length, 128), 0)
    lane = lax.broadcasted_iota(jnp.int32, (length, 128), 1)
    kx_ref[:, 128:] = jnp.where(lane % 64 == row // POOL, F32(1.0), F32(0.0)).astype(BF16)
    sum_ref[...] = jnp.zeros_like(sum_ref)

    size = 256
    pieces = [slice(c * size, (c + 1) * size) for c in range(length // size)]
    fold = (size // 8, 8, 512)

    def scores(b, i):
        top = None
        for r in pieces:
            part = nt(kx_ref[r, :], qx_ref[i])
            s_ref[b, r, :] = part
            part = jnp.max(part.reshape(fold), axis=0)
            top = part if top is None else jnp.maximum(top, part)
        return jnp.max(top, axis=0, keepdims=True)

    def weigh(b, i, top):
        total = mean = jnp.zeros((8, 512), F32)
        for r in pieces:
            weights = jnp.exp2((s_ref[b, r, :] - top) * (scale * F32(1.4426950408889634)))
            slope = nt(v_ref[r, :], pack_ref[i, :512, :])
            s_ref[b, r, :] = weights
            sl_ref[b, r, :] = slope
            total += jnp.sum(weights.reshape(fold), axis=0)
            mean += jnp.sum((weights * slope).reshape(fold), axis=0)
        inverse = 1.0 / jnp.sum(total, axis=0, keepdims=True)
        return inverse, jnp.sum(mean, axis=0, keepdims=True) * inverse

    def products(b, i, inverse, mean):
        query, grad = qx_ref[i][:, :128], pack_ref[i, :512, :]
        for r in pieces:
            probs = s_ref[b, r, :] * inverse
            probs_b = probs.astype(BF16)
            centred_b = (probs * (sl_ref[b, r, :] - mean)).astype(BF16)
            pb_ref[b, r, :] = probs_b
            cb_ref[b, r, :] = centred_b
            sum_ref[r, :128] += nn(centred_b, query)
            sum_ref[r, 128:] += nn(probs_b, grad)
        attended = nn(vt_ref[...], pb_ref[b]).astype(BF16)
        grad_q = (nn(kt_ref[...], cb_ref[b]) * scale).astype(BF16)
        for h in range(4):
            here = slice(128 * h, 128 * h + 128)
            att_ref[i, here, :] = attended[:, here]
            gq_ref[i, here, :] = grad_q[:, here]

    def step(part, carry):
        start = part * RUN
        stats = weigh(0, start, scores(0, start))
        for d in range(RUN):
            last = d == RUN - 1
            top = None if last else scores((d + 1) % 2, start + d + 1)
            products(d % 2, start + d, *stats)
            if not last:
                stats = weigh((d + 1) % 2, start + d + 1, top)
        return carry

    lax.fori_loop(0, count // RUN, step, 0)
    side = lax.broadcasted_iota(jnp.int32, (128, 256), 1)
    for s in range(count):
        level = pack_ref[s, 1024:1025, 0:1].astype(F32) * CLIP_LEVEL
        inside = jnp.abs(kv_ref[s, :, :256].astype(F32)) <= level
        part = sum_ref[128 * s : 128 * s + 128, :]
        part = jnp.where(side < 128, part * scale, part)
        out_ref[s] = jnp.where(inside, part, 0.0).astype(BF16)


def output_body(me_ref, trunk_ref, att_ref, wout_ref, out_ref):
    me = me_ref[0]
    total = trunk_ref[...].astype(F32)
    for h in range(4):
        here = slice(128 * h, 128 * h + 128)
        total += nn(att_ref[me, here, :].astype(F32).T.astype(BF16), wout_ref[here, :])
    out_ref[...] = total.astype(BF16)


def back_body(
    dil_ref, me_ref, x_ref, att_ref, gq_ref, gkv_ref, wq_ref, wkv_ref, taps_ref, slope_ref,
    out_ref, g_ref, turn_ref,
):
    offset = take_taps(me_ref[0], taps_ref, turn_ref)
    count, channels, _ = g_ref.shape
    mine = pl.ds(pl.multiple_of(me_ref[0] * channels, 16), channels)
    my_wq, my_wkv = wq_ref[mine, :], wkv_ref[mine, :]
    grad_out = jnp.zeros((channels, 512), F32)
    for s in range(count):
        turned = x_ref[s, channels:, :]
        g_ref[s] = turned.astype(F32) + nn(my_wq, gq_ref[s]) + nt(my_wkv, gkv_ref[s])
        grad_out += nt(turned, att_ref[s])
    half = channels // 2
    for s in range(count):
        cols = grad_out[:, 64 * s : 64 * s + 64]
        out_ref[s, channels:, :] = jnp.concatenate([cols[:half], cols[half:]], axis=1).astype(BF16)

    def chunk(c, carry):
        rows = pl.ds(pl.multiple_of(c * 16, 16), 16)
        flow = [g_ref[s, rows, :] for s in range(count)]
        tap = turn_ref[pl.ds(pl.multiple_of(offset + c * 16, 16), 16), :]
        for layer in (1, 0):
            t0, t1, t2 = (tap[:, 8 * layer + k : 8 * layer + k + 1] for k in range(3))
            pushed = [
                (flow[s] * slope_ref[layer, s, rows, :].astype(F32)).astype(BF16).astype(F32)
                for s in range(count)
            ]
            before, after = shifts(pushed, dil_ref[layer])
            flow = [
                flow[s] + t0 * after[s] + t1 * pushed[s] + t2 * before[s] for s in range(count)
            ]
        for s in range(count):
            out_ref[s, rows, :] = flow[s].astype(BF16)
        return carry

    lax.fori_loop(0, channels // 16, chunk, 0)


def weights_body(x_ref, gq_ref, gkv_ref, gq_out_ref, gkv_out_ref):
    count, channels, _ = x_ref.shape
    first = jnp.zeros(gq_out_ref.shape, F32)
    second = jnp.zeros(gkv_out_ref.shape, F32)
    for s in range(count):
        first += nt(x_ref[s], gq_ref[s])
        second += nn(x_ref[s], gkv_ref[s])
    gq_out_ref[...] = first.astype(BF16)
    gkv_out_ref[...] = second.astype(BF16)


def last_body(x_ref, grad_ref, gout_ref):
    count, wide, _ = x_ref.shape
    channels = grad_ref.shape[1] // count
    half = wide - channels
    for s in range(count):
        grad_ref[:, s * channels : (s + 1) * channels] = (
            x_ref[s, :channels, :].astype(F32).T.astype(BF16)
        )
        turned = x_ref[s, channels:, :].astype(F32).T.astype(BF16)
        gout_ref[:, s * channels : s * channels + half] = turned[:64]
        gout_ref[:, s * channels + half : (s + 1) * channels] = turned[64:]


def local(tokens, dilations, taps, w_query, w_keyval, w_out, exponents, pair, w_bias, cotangent):
    count = lax.axis_size("seq")
    me = lax.axis_index("seq")
    rows, width = tokens.shape
    ch = width // count
    length = rows * count
    place = me.astype(jnp.int32).reshape(1)
    blocks = (count, ch, rows)

    turned_shape = (count, 2 * ch, rows)
    (first,) = call(
        flip_body,
        [(turned_shape, BF16)],
        "flip",
        0,
        4 * rows * width,
        scratch=[
            pltpu.VMEM((rows, width), BF16),
            pltpu.VMEM((rows, width), BF16),
            pltpu.VMEM(turned_shape, BF16),
            pltpu.SemaphoreType.DMA((count + 2,)),
        ],
        limit=63,
        space=ANY,
    )(tokens, cotangent)
    turned = exchange(first)
    (grad_attn,) = call(
        early_body, [((576, 128), BF16)], "early", 2 * rows * width * 512, 4 * MIB
    )(exponents, cotangent, w_out, pair, w_bias.T)
    my_taps = jnp.transpose(taps, (1, 0, 2))
    turn = pltpu.VMEM((256, 16), F32)
    across = [(i, (i + 4) % 8) for i in range(8)]
    around = {o: [(i, i // 4 * 4 + (i + o) % 4) for i in range(8)] for o in (1, 2, 3)}
    columns = [grad_attn] + [lax.ppermute(grad_attn, "seq", around[o]) for o in (1, 3, 2)]

    other = [lax.ppermute(grad_attn, "seq", across)]

    trunk_turned, slopes = call(
        conv_body,
        [(blocks, BF16), ((2, *blocks), BF16)],
        "conv",
        100 * length * ch,
        4 * MIB,
        scratch=[turn],
        limit=CONV_LIMIT,
    )(dilations, place, after(turned, grad_attn), my_taps)
    back = exchange(after(trunk_turned, *columns, *other))
    other += [lax.ppermute(c, "seq", across) for c in columns[1:3]]
    other += [lax.ppermute(other[0], "seq", around[2])]

    keyval, trunk = call(
        keyval_body,
        [((count, rows, 768), BF16), ((rows, width), BF16)],
        "keyval",
        2 * rows * width * 768,
        2 * MIB,
    )(exponents, back, w_keyval, w_query)
    keyval = exchange(after(keyval, *other))
    columns = columns + other
    (pack,) = call(
        query_body,
        [((count, 1040, 128), BF16)],
        "query",
        2 * rows * width * 512,
        3 * MIB,
        scratch=[pltpu.VMEM((count, 64, 128), BF16)],
    )(place, *columns)

    heads = (count, 512, 128)
    attended, grad_q, grad_kv = call(
        attention_body,
        [(heads, BF16), (heads, BF16), ((count, rows, 256), BF16)],
        "attention",
        12 * length * length * 512,
        8 * MIB,
        scratch=[
            pltpu.VMEM((length, 256), F32),
            pltpu.VMEM((length, 256), BF16),
            pltpu.VMEM((length, 128), BF16),
            pltpu.VMEM((128, length), BF16),
            pltpu.VMEM((128, length), BF16),
            pltpu.VMEM((count, 512, 256), BF16),
            pltpu.VMEM((2, length, 512), F32),
            pltpu.VMEM((2, length, 512), F32),
            pltpu.VMEM((2, length, 512), BF16),
            pltpu.VMEM((2, length, 512), BF16),
        ],
        limit=32,
    )(keyval, pack)

    (final,) = call(
        back_body,
        [((count, ch + ch // 2, rows), BF16)],
        "back",
        2 * length * ch * 1280,
        8 * MIB,
        scratch=[pltpu.VMEM(blocks, F32), turn],
    )(dilations, place, turned, attended, grad_q, grad_kv, w_query, w_keyval, my_taps, slopes)
    final = exchange(final)
    grad_query, grad_keyval = call(
        weights_body,
        [((ch, 512), BF16), ((ch, 256), BF16)],
        "weights",
        2 * length * ch * 768,
        4 * MIB,
    )(trunk_turned, grad_q, grad_kv)
    (output,) = call(output_body, [((rows, width), BF16)], "output", 2 * rows * width * 512, 3 * MIB)(
        place, trunk, attended, w_out
    )
    grad_tokens, grad_out = call(
        last_body, [((rows, width), BF16), ((64, width), BF16)], "last", 0, 2 * MIB
    )(final)
    return output, grad_tokens, grad_query, grad_keyval, grad_out


def solution(mesh):
    both = P(("dp", "seq"))
    in_specs = (both, P(), P(), P(), P(), P(), both, both, P(), both)
    return jax.shard_map(
        local, mesh=mesh, in_specs=in_specs, out_specs=(both,) * 5, check_vma=False
    )
```

```python
import jax
import jax.numpy as jnp
from jax import lax
from jax.experimental import pallas as pl
from jax.experimental.pallas import tpu as pltpu
from jax.sharding import PartitionSpec as P

POOL = 16
CLIP_LEVEL = 448.0
RUN = 8
CONV_LIMIT = 63
F32 = jnp.float32
BF16 = jnp.bfloat16
MIB = 1 << 20
VMEM = pl.BlockSpec(memory_space=pltpu.VMEM)
SMEM = pl.BlockSpec(memory_space=pltpu.SMEM)
ANY = pl.BlockSpec(memory_space=pl.ANY)


def nn(a, b):
    return jnp.dot(a, b, preferred_element_type=F32)


def nt(a, b):
    return lax.dot_general(a, b, (((1,), (1,)), ((), ())), preferred_element_type=F32)


def call(body, outs, name, flops=0, nbytes=0, scratch=(), limit=16, space=VMEM):
    def run(*args):
        return pl.pallas_call(
            body,
            out_shape=[jax.ShapeDtypeStruct(s, d) for s, d in outs],
            in_specs=[SMEM if a.dtype == jnp.int32 else space for a in args],
            out_specs=[space] * len(outs),
            scratch_shapes=list(scratch),
            compiler_params=pltpu.CompilerParams(vmem_limit_bytes=limit * MIB),
            cost_estimate=pl.CostEstimate(flops=flops, bytes_accessed=nbytes, transcendentals=0),
            name=name,
        )(*args)

    return run


def exchange(x):
    return lax.all_to_all(x, "seq", split_axis=0, concat_axis=0, tiled=True)


def after(x, *others):
    return lax.optimization_barrier((x, *others))[0]


def flip_body(tok_hbm, cot_hbm, out_hbm, tok_ref, cot_ref, out_ref, sems):
    n, rows, _ = out_ref.shape
    half = rows // 2
    reads = [
        pltpu.make_async_copy(tok_hbm, tok_ref, sems.at[n]),
        pltpu.make_async_copy(cot_hbm, cot_ref, sems.at[n + 1]),
    ]
    for copy in reads:
        copy.start()
    reads[0].wait()
    for r in range(n):
        out_ref[r, :half, :] = tok_ref[:, r * half : (r + 1) * half].astype(F32).T.astype(BF16)
    reads[1].wait()
    writes = []
    for r in range(n):
        out_ref[r, half:, :] = cot_ref[:, r * half : (r + 1) * half].astype(F32).T.astype(BF16)
        writes.append(pltpu.make_async_copy(out_ref.at[r], out_hbm.at[r], sems.at[r]))
        writes[r].start()
    for copy in writes:
        copy.wait()


def split3(x):
    hi = x.astype(BF16)
    rest = x - hi.astype(F32)
    mid = rest.astype(BF16)
    lo = (rest - mid.astype(F32)).astype(BF16)
    return hi, mid, lo


def take_taps(me, taps_ref, turn_ref):
    begin = me * 192
    window = begin // 128 * 128
    for k in range(3):
        part = taps_ref[k, :, pl.ds(pl.multiple_of(window, 128), 256)]
        for layer in range(2):
            turn_ref[:, 8 * layer + k : 8 * layer + k + 1] = part[layer : layer + 1, :].T
    return begin - window


def early_body(exp_ref, cot_ref, wout_ref, pair_ref, wb_ref, out_ref):
    weights = jnp.concatenate([wb_ref[...], wb_ref[...]], axis=0).T
    lane = lax.broadcasted_iota(jnp.int32, (128, 128), 1)
    head = (lane % 32) // 8
    wide = jnp.zeros((128, 128), F32)
    for h in range(4):
        wide = jnp.where(head == h, weights[:, h : h + 1], wide)
    pieces = split3(wide)
    cells = jnp.zeros((64, 128), F32)
    for j in range(8):
        pick = lane % 8 == j
        for piece in pieces:
            cells += nn(pair_ref[j], jnp.where(pick, piece.astype(F32), 0.0).astype(BF16))
    hi, mid, lo = (piece.astype(F32) for piece in split3(cells))
    group = lax.broadcasted_iota(jnp.int32, (64, 128), 1) // 32
    factor, _ = power_of_two(exp_ref[0])
    packed = jnp.where(group == 0, hi, jnp.where(group == 1, mid, jnp.where(group == 2, lo, factor)))
    out_ref[512:, :] = packed.astype(BF16)
    grad = nt(cot_ref[...], wout_ref[...]).astype(BF16)
    for h in range(4):
        out_ref[128 * h : 128 * h + 128, :] = grad[:, 128 * h : 128 * h + 128]


def sigmoid(v):
    return 0.5 * jnp.tanh(0.5 * v) + 0.5


def shifts(blocks, d):
    lane = lax.broadcasted_iota(jnp.int32, blocks[0].shape, 1)
    turn = lax.rem(d, 128)
    back = 128 - d
    rolled = [pltpu.roll(b, turn, 1) for b in blocks]
    other = [pltpu.roll(b, back, 1) for b in blocks]
    zero = jnp.zeros_like(blocks[0])
    count = len(blocks)
    before = [
        jnp.where(lane < d, rolled[s - 1] if s else zero, rolled[s]) for s in range(count)
    ]
    after = [
        jnp.where(lane >= back, other[s + 1] if s + 1 < count else zero, other[s])
        for s in range(count)
    ]
    return before, after


def conv_body(dil_ref, me_ref, x_ref, taps_ref, out_ref, slope_ref, turn_ref):
    offset = take_taps(me_ref[0], taps_ref, turn_ref)
    count, channels, _ = out_ref.shape

    def chunk(c, carry):
        rows = pl.ds(pl.multiple_of(c * 16, 16), 16)
        cur = [x_ref[s, rows, :].astype(F32) for s in range(count)]
        tap = turn_ref[pl.ds(pl.multiple_of(offset + c * 16, 16), 16), :]
        for layer in range(2):
            t0, t1, t2 = (tap[:, 8 * layer + k : 8 * layer + k + 1] for k in range(3))
            before, after = shifts(cur, dil_ref[layer])
            for s in range(count):
                mixed = t0 * before[s] + t1 * cur[s] + t2 * after[s]
                sigma = sigmoid(mixed)
                gated = mixed * sigma
                slope_ref[layer, s, rows, :] = (sigma + gated * (1.0 - sigma)).astype(BF16)
                cur[s] = (cur[s] + gated).astype(BF16).astype(F32)
        for s in range(count):
            out_ref[s, rows, :] = cur[s].astype(BF16)
        return carry

    lax.fori_loop(0, channels // 16, chunk, 0)


def power_of_two(e):
    up, down = F32(1.0), F32(1.0)
    size = jnp.abs(e)
    for bit in range(6):
        on = ((size >> bit) & 1) == 1
        up = up * jnp.where(on, F32(2.0 ** (1 << bit)), F32(1.0))
        down = down * jnp.where(on, F32(0.5 ** (1 << bit)), F32(1.0))
    return jnp.where(e >= 0, up, down), jnp.where(e >= 0, down, up)


def keyval_body(exp_ref, x_ref, wkv_ref, wq_ref, send_ref, trunk_ref):
    count, channels, _ = x_ref.shape
    for s in range(count):
        trunk_ref[:, s * channels : (s + 1) * channels] = x_ref[s].astype(F32).T.astype(BF16)
    factor, inverse = power_of_two(exp_ref[0])
    unscaled = nn(trunk_ref[...], wkv_ref[...]) * inverse
    codes = jnp.clip(unscaled, -CLIP_LEVEL, CLIP_LEVEL).astype(BF16).astype(F32)
    marked = jnp.where(
        jnp.abs(unscaled) < CLIP_LEVEL, codes, jnp.where(unscaled > 0.0, F32(512.0), F32(-512.0))
    )
    marked = (marked * factor).astype(BF16)
    query = nn(trunk_ref[...], wq_ref[...]).astype(BF16)
    for s in range(count):
        send_ref[s, :, :256] = marked
        send_ref[s, :, 256:] = query


def query_body(me_ref, *refs):
    columns, (pack_ref, cells_ref) = refs[:8], refs[8:]
    me = me_ref[0]
    x, y = me // 4, lax.rem(me, 4)
    count = cells_ref.shape[0]
    for k, ref in enumerate(columns):
        block = (x if k < 4 else 1 - x) * 4 + lax.rem(y + (0, 3, 1, 2)[k % 4], 4)
        cells_ref[block] = ref[512:, :]
        pack_ref[block, :512, :] = ref[:512, :]
    row = lax.broadcasted_iota(jnp.int32, (128, 512), 0)
    col = lax.broadcasted_iota(jnp.int32, (128, 512), 1)
    same_head = (row % 32) // 8 == col // 128
    target = (row % 8) - (col % 64)
    mirrored = jnp.zeros((64, 512), F32)
    for s in range(count):
        pick = jnp.where(same_head & (row < 96) & (target == -8 * s), F32(1.0), F32(0.0))
        mirrored += nn(cells_ref[s], pick.astype(BF16))
    lane = lax.broadcasted_iota(jnp.int32, (64, 128), 1)
    for h in range(4):
        one = mirrored[:, 128 * h : 128 * h + 128]
        other = jnp.concatenate([one, one], axis=0).T
        bias = 0.5 * (one + other[:64, :]) * F32(128.0**0.5)
        hi = bias.astype(BF16).astype(F32)
        both = jnp.where(lane < 64, hi, bias - hi).astype(BF16)
        for s in range(count):
            wide = both[8 * s : 8 * s + 8].astype(F32)
            wide = jnp.broadcast_to(wide[:, None, :], (8, POOL, 128)).reshape(128, 128)
            pack_ref[s, 512 + 128 * h : 640 + 128 * h, :] = wide.astype(BF16)
    for s in range(count):
        corner = cells_ref[s, 0:1, 127:128].astype(F32)
        pack_ref[s, 1024:, :] = jnp.broadcast_to(corner, (16, 128)).astype(BF16)


def attention_body(
    kv_ref, pack_ref, att_ref, gq_ref, out_ref,
    sum_ref, kx_ref, v_ref, kt_ref, vt_ref, qx_ref, s_ref, sl_ref, pb_ref, cb_ref,
):
    scale = F32(128.0**-0.5)
    count = kv_ref.shape[0]
    length = count * 128
    for s in range(count):
        rows = slice(128 * s, 128 * s + 128)
        level = pack_ref[s, 1024:1025, 0:1].astype(F32) * CLIP_LEVEL
        plain = jnp.clip(kv_ref[s, :, :256].astype(F32), -level, level)
        kx_ref[rows, :128] = plain[:, :128].astype(BF16)
        v_ref[rows, :] = plain[:, 128:].astype(BF16)
        kt_ref[:, rows] = plain[:, :128].T.astype(BF16)
        vt_ref[:, rows] = plain[:, 128:].T.astype(BF16)
        for h in range(4):
            here = slice(128 * h, 128 * h + 128)
            qx_ref[s, here, :128] = kv_ref[s, :, 256 + 128 * h : 384 + 128 * h]
            qx_ref[s, here, 128:] = pack_ref[s, 512 + 128 * h : 640 + 128 * h, :]
    row = lax.broadcasted_iota(jnp.int32, (length, 128), 0)
    lane = lax.broadcasted_iota(jnp.int32, (length, 128), 1)
    kx_ref[:, 128:] = jnp.where(lane % 64 == row // POOL, F32(1.0), F32(0.0)).astype(BF16)
    sum_ref[...] = jnp.zeros_like(sum_ref)

    size = 256
    pieces = [slice(c * size, (c + 1) * size) for c in range(length // size)]
    fold = (size // 8, 8, 512)

    def scores(b, i):
        top = None
        for r in pieces:
            part = nt(kx_ref[r, :], qx_ref[i])
            s_ref[b, r, :] = part
            part = jnp.max(part.reshape(fold), axis=0)
            top = part if top is None else jnp.maximum(top, part)
        return jnp.max(top, axis=0, keepdims=True)

    def weigh(b, i, top):
        total = mean = jnp.zeros((8, 512), F32)
        for r in pieces:
            weights = jnp.exp2((s_ref[b, r, :] - top) * (scale * F32(1.4426950408889634)))
            slope = nt(v_ref[r, :], pack_ref[i, :512, :])
            s_ref[b, r, :] = weights
            sl_ref[b, r, :] = slope
            total += jnp.sum(weights.reshape(fold), axis=0)
            mean += jnp.sum((weights * slope).reshape(fold), axis=0)
        inverse = 1.0 / jnp.sum(total, axis=0, keepdims=True)
        return inverse, jnp.sum(mean, axis=0, keepdims=True) * inverse

    def products(b, i, inverse, mean):
        query, grad = qx_ref[i][:, :128], pack_ref[i, :512, :]
        for r in pieces:
            probs = s_ref[b, r, :] * inverse
            probs_b = probs.astype(BF16)
            centred_b = (probs * (sl_ref[b, r, :] - mean)).astype(BF16)
            pb_ref[b, r, :] = probs_b
            cb_ref[b, r, :] = centred_b
            sum_ref[r, :128] += nn(centred_b, query)
            sum_ref[r, 128:] += nn(probs_b, grad)
        attended = nn(vt_ref[...], pb_ref[b]).astype(BF16)
        grad_q = (nn(kt_ref[...], cb_ref[b]) * scale).astype(BF16)
        for h in range(4):
            here = slice(128 * h, 128 * h + 128)
            att_ref[i, here, :] = attended[:, here]
            gq_ref[i, here, :] = grad_q[:, here]

    def step(part, carry):
        start = part * RUN
        stats = weigh(0, start, scores(0, start))
        for d in range(RUN):
            last = d == RUN - 1
            top = None if last else scores((d + 1) % 2, start + d + 1)
            products(d % 2, start + d, *stats)
            if not last:
                stats = weigh((d + 1) % 2, start + d + 1, top)
        return carry

    lax.fori_loop(0, count // RUN, step, 0)
    side = lax.broadcasted_iota(jnp.int32, (128, 256), 1)
    for s in range(count):
        level = pack_ref[s, 1024:1025, 0:1].astype(F32) * CLIP_LEVEL
        inside = jnp.abs(kv_ref[s, :, :256].astype(F32)) <= level
        part = sum_ref[128 * s : 128 * s + 128, :]
        part = jnp.where(side < 128, part * scale, part)
        out_ref[s] = jnp.where(inside, part, 0.0).astype(BF16)


def output_body(me_ref, trunk_ref, att_ref, wout_ref, out_ref):
    me = me_ref[0]
    total = trunk_ref[...].astype(F32)
    for h in range(4):
        here = slice(128 * h, 128 * h + 128)
        total += nn(att_ref[me, here, :].astype(F32).T.astype(BF16), wout_ref[here, :])
    out_ref[...] = total.astype(BF16)


def back_body(
    dil_ref, me_ref, x_ref, att_ref, gq_ref, gkv_ref, wq_ref, wkv_ref, taps_ref, slope_ref,
    out_ref, g_ref, turn_ref,
):
    offset = take_taps(me_ref[0], taps_ref, turn_ref)
    count, channels, _ = g_ref.shape
    mine = pl.ds(pl.multiple_of(me_ref[0] * channels, 16), channels)
    my_wq, my_wkv = wq_ref[mine, :], wkv_ref[mine, :]
    grad_out = jnp.zeros((channels, 512), F32)
    for s in range(count):
        turned = x_ref[s, channels:, :]
        g_ref[s] = turned.astype(F32) + nn(my_wq, gq_ref[s]) + nt(my_wkv, gkv_ref[s])
        grad_out += nt(turned, att_ref[s])
    half = channels // 2
    for s in range(count):
        cols = grad_out[:, 64 * s : 64 * s + 64]
        out_ref[s, channels:, :] = jnp.concatenate([cols[:half], cols[half:]], axis=1).astype(BF16)

    def chunk(c, carry):
        rows = pl.ds(pl.multiple_of(c * 16, 16), 16)
        flow = [g_ref[s, rows, :] for s in range(count)]
        tap = turn_ref[pl.ds(pl.multiple_of(offset + c * 16, 16), 16), :]
        for layer in (1, 0):
            t0, t1, t2 = (tap[:, 8 * layer + k : 8 * layer + k + 1] for k in range(3))
            pushed = [
                (flow[s] * slope_ref[layer, s, rows, :].astype(F32)).astype(BF16).astype(F32)
                for s in range(count)
            ]
            before, after = shifts(pushed, dil_ref[layer])
            flow = [
                flow[s] + t0 * after[s] + t1 * pushed[s] + t2 * before[s] for s in range(count)
            ]
        for s in range(count):
            out_ref[s, rows, :] = flow[s].astype(BF16)
        return carry

    lax.fori_loop(0, channels // 16, chunk, 0)


def weights_body(x_ref, gq_ref, gkv_ref, gq_out_ref, gkv_out_ref):
    count, channels, _ = x_ref.shape
    first = jnp.zeros(gq_out_ref.shape, F32)
    second = jnp.zeros(gkv_out_ref.shape, F32)
    for s in range(count):
        first += nt(x_ref[s], gq_ref[s])
        second += nn(x_ref[s], gkv_ref[s])
    gq_out_ref[...] = first.astype(BF16)
    gkv_out_ref[...] = second.astype(BF16)


def last_body(x_ref, grad_ref, gout_ref):
    count, wide, _ = x_ref.shape
    channels = grad_ref.shape[1] // count
    half = wide - channels
    for s in range(count):
        grad_ref[:, s * channels : (s + 1) * channels] = (
            x_ref[s, :channels, :].astype(F32).T.astype(BF16)
        )
        turned = x_ref[s, channels:, :].astype(F32).T.astype(BF16)
        gout_ref[:, s * channels : s * channels + half] = turned[:64]
        gout_ref[:, s * channels + half : (s + 1) * channels] = turned[64:]


def local(tokens, dilations, taps, w_query, w_keyval, w_out, exponents, pair, w_bias, cotangent):
    count = lax.axis_size("seq")
    me = lax.axis_index("seq")
    rows, width = tokens.shape
    ch = width // count
    length = rows * count
    place = me.astype(jnp.int32).reshape(1)
    blocks = (count, ch, rows)

    turned_shape = (count, 2 * ch, rows)
    (first,) = call(
        flip_body,
        [(turned_shape, BF16)],
        "flip",
        0,
        4 * rows * width,
        scratch=[
            pltpu.VMEM((rows, width), BF16),
            pltpu.VMEM((rows, width), BF16),
            pltpu.VMEM(turned_shape, BF16),
            pltpu.SemaphoreType.DMA((count + 2,)),
        ],
        limit=63,
        space=ANY,
    )(tokens, cotangent)
    turned = exchange(first)
    (grad_attn,) = call(
        early_body, [((576, 128), BF16)], "early", 2 * rows * width * 512, 4 * MIB
    )(exponents, cotangent, w_out, pair, w_bias.T)
    my_taps = jnp.transpose(taps, (1, 0, 2))
    turn = pltpu.VMEM((256, 16), F32)
    across = [(i, (i + 4) % 8) for i in range(8)]
    around = {o: [(i, i // 4 * 4 + (i + o) % 4) for i in range(8)] for o in (1, 2, 3)}
    columns = [grad_attn] + [lax.ppermute(grad_attn, "seq", around[o]) for o in (1, 3, 2)]

    other = [lax.ppermute(grad_attn, "seq", across)]

    trunk_turned, slopes = call(
        conv_body,
        [(blocks, BF16), ((2, *blocks), BF16)],
        "conv",
        100 * length * ch,
        4 * MIB,
        scratch=[turn],
        limit=CONV_LIMIT,
    )(dilations, place, after(turned, grad_attn), my_taps)
    back = exchange(after(trunk_turned, *columns, *other))
    other += [lax.ppermute(c, "seq", across) for c in columns[1:3]]
    other += [lax.ppermute(other[0], "seq", around[2])]

    keyval, trunk = call(
        keyval_body,
        [((count, rows, 768), BF16), ((rows, width), BF16)],
        "keyval",
        2 * rows * width * 768,
        2 * MIB,
    )(exponents, back, w_keyval, w_query)
    keyval = exchange(after(keyval, *other))
    columns = columns + other
    (pack,) = call(
        query_body,
        [((count, 1040, 128), BF16)],
        "query",
        2 * rows * width * 512,
        3 * MIB,
        scratch=[pltpu.VMEM((count, 64, 128), BF16)],
    )(place, *columns)

    heads = (count, 512, 128)
    attended, grad_q, grad_kv = call(
        attention_body,
        [(heads, BF16), (heads, BF16), ((count, rows, 256), BF16)],
        "attention",
        12 * length * length * 512,
        8 * MIB,
        scratch=[
            pltpu.VMEM((length, 256), F32),
            pltpu.VMEM((length, 256), BF16),
            pltpu.VMEM((length, 128), BF16),
            pltpu.VMEM((128, length), BF16),
            pltpu.VMEM((128, length), BF16),
            pltpu.VMEM((count, 512, 256), BF16),
            pltpu.VMEM((2, length, 512), F32),
            pltpu.VMEM((2, length, 512), F32),
            pltpu.VMEM((2, length, 512), BF16),
            pltpu.VMEM((2, length, 512), BF16),
        ],
        limit=32,
    )(keyval, pack)

    (final,) = call(
        back_body,
        [((count, ch + ch // 2, rows), BF16)],
        "back",
        2 * length * ch * 1280,
        8 * MIB,
        scratch=[pltpu.VMEM(blocks, F32), turn],
    )(dilations, place, turned, attended, grad_q, grad_kv, w_query, w_keyval, my_taps, slopes)
    final = exchange(final)
    grad_query, grad_keyval = call(
        weights_body,
        [((ch, 512), BF16), ((ch, 256), BF16)],
        "weights",
        2 * length * ch * 768,
        4 * MIB,
    )(trunk_turned, grad_q, grad_kv)
    (output,) = call(output_body, [((rows, width), BF16)], "output", 2 * rows * width * 512, 3 * MIB)(
        place, trunk, attended, w_out
    )
    grad_tokens, grad_out = call(
        last_body, [((rows, width), BF16), ((64, width), BF16)], "last", 0, 2 * MIB
    )(final)
    return output, grad_tokens, grad_query, grad_keyval, grad_out


def solution(mesh):
    both = P(("dp", "seq"))
    in_specs = (both, P(), P(), P(), P(), P(), both, both, P(), both)
    return jax.shard_map(
        local, mesh=mesh, in_specs=in_specs, out_specs=(both,) * 5, check_vma=False
    )
```

```python
import jax
import jax.numpy as jnp
from jax import lax
from jax.experimental import pallas as pl
from jax.experimental.pallas import tpu as pltpu
from jax.sharding import PartitionSpec as P

POOL = 16
CLIP_LEVEL = 448.0
RUN = 8
CONV_LIMIT = 63
F32 = jnp.float32
BF16 = jnp.bfloat16
MIB = 1 << 20
VMEM = pl.BlockSpec(memory_space=pltpu.VMEM)
SMEM = pl.BlockSpec(memory_space=pltpu.SMEM)
ANY = pl.BlockSpec(memory_space=pl.ANY)


def nn(a, b):
    return jnp.dot(a, b, preferred_element_type=F32)


def nt(a, b):
    return lax.dot_general(a, b, (((1,), (1,)), ((), ())), preferred_element_type=F32)


def call(body, outs, name, flops=0, nbytes=0, scratch=(), limit=16, space=VMEM):
    def run(*args):
        return pl.pallas_call(
            body,
            out_shape=[jax.ShapeDtypeStruct(s, d) for s, d in outs],
            in_specs=[SMEM if a.dtype == jnp.int32 else space for a in args],
            out_specs=[space] * len(outs),
            scratch_shapes=list(scratch),
            compiler_params=pltpu.CompilerParams(vmem_limit_bytes=limit * MIB),
            cost_estimate=pl.CostEstimate(flops=flops, bytes_accessed=nbytes, transcendentals=0),
            name=name,
        )(*args)

    return run


def exchange(x):
    return lax.all_to_all(x, "seq", split_axis=0, concat_axis=0, tiled=True)


def after(x, *others):
    return lax.optimization_barrier((x, *others))[0]


def flip_body(tok_hbm, cot_hbm, out_hbm, tok_ref, cot_ref, out_ref, sems):
    n, rows, _ = out_ref.shape
    half = rows // 2
    reads = [
        pltpu.make_async_copy(tok_hbm, tok_ref, sems.at[n]),
        pltpu.make_async_copy(cot_hbm, cot_ref, sems.at[n + 1]),
    ]
    for copy in reads:
        copy.start()
    reads[0].wait()
    for r in range(n):
        out_ref[r, :half, :] = tok_ref[:, r * half : (r + 1) * half].astype(F32).T.astype(BF16)
    reads[1].wait()
    writes = []
    for r in range(n):
        out_ref[r, half:, :] = cot_ref[:, r * half : (r + 1) * half].astype(F32).T.astype(BF16)
        writes.append(pltpu.make_async_copy(out_ref.at[r], out_hbm.at[r], sems.at[r]))
        writes[r].start()
    for copy in writes:
        copy.wait()


def split3(x):
    hi = x.astype(BF16)
    rest = x - hi.astype(F32)
    mid = rest.astype(BF16)
    lo = (rest - mid.astype(F32)).astype(BF16)
    return hi, mid, lo


def take_taps(me, taps_ref, turn_ref):
    begin = me * 192
    window = begin // 128 * 128
    for k in range(3):
        part = taps_ref[k, :, pl.ds(pl.multiple_of(window, 128), 256)]
        for layer in range(2):
            turn_ref[:, 8 * layer + k : 8 * layer + k + 1] = part[layer : layer + 1, :].T
    return begin - window


def early_body(exp_ref, cot_ref, wout_ref, pair_ref, wb_ref, out_ref):
    weights = jnp.concatenate([wb_ref[...], wb_ref[...]], axis=0).T
    lane = lax.broadcasted_iota(jnp.int32, (128, 128), 1)
    head = (lane % 32) // 8
    wide = jnp.zeros((128, 128), F32)
    for h in range(4):
        wide = jnp.where(head == h, weights[:, h : h + 1], wide)
    pieces = split3(wide)
    cells = jnp.zeros((64, 128), F32)
    for j in range(8):
        pick = lane % 8 == j
        for piece in pieces:
            cells += nn(pair_ref[j], jnp.where(pick, piece.astype(F32), 0.0).astype(BF16))
    hi, mid, lo = (piece.astype(F32) for piece in split3(cells))
    group = lax.broadcasted_iota(jnp.int32, (64, 128), 1) // 32
    factor, _ = power_of_two(exp_ref[0])
    packed = jnp.where(group == 0, hi, jnp.where(group == 1, mid, jnp.where(group == 2, lo, factor)))
    out_ref[512:, :] = packed.astype(BF16)
    grad = nt(cot_ref[...], wout_ref[...]).astype(BF16)
    for h in range(4):
        out_ref[128 * h : 128 * h + 128, :] = grad[:, 128 * h : 128 * h + 128]


def sigmoid(v):
    return 0.5 * jnp.tanh(0.5 * v) + 0.5


def shifts(blocks, d):
    lane = lax.broadcasted_iota(jnp.int32, blocks[0].shape, 1)
    turn = lax.rem(d, 128)
    back = 128 - d
    rolled = [pltpu.roll(b, turn, 1) for b in blocks]
    other = [pltpu.roll(b, back, 1) for b in blocks]
    zero = jnp.zeros_like(blocks[0])
    count = len(blocks)
    before = [
        jnp.where(lane < d, rolled[s - 1] if s else zero, rolled[s]) for s in range(count)
    ]
    after = [
        jnp.where(lane >= back, other[s + 1] if s + 1 < count else zero, other[s])
        for s in range(count)
    ]
    return before, after


def conv_body(dil_ref, me_ref, x_ref, taps_ref, out_ref, slope_ref, turn_ref):
    offset = take_taps(me_ref[0], taps_ref, turn_ref)
    count, channels, _ = out_ref.shape

    def chunk(c, carry):
        rows = pl.ds(pl.multiple_of(c * 16, 16), 16)
        cur = [x_ref[s, rows, :].astype(F32) for s in range(count)]
        tap = turn_ref[pl.ds(pl.multiple_of(offset + c * 16, 16), 16), :]
        for layer in range(2):
            t0, t1, t2 = (tap[:, 8 * layer + k : 8 * layer + k + 1] for k in range(3))
            before, after = shifts(cur, dil_ref[layer])
            for s in range(count):
                mixed = t0 * before[s] + t1 * cur[s] + t2 * after[s]
                sigma = sigmoid(mixed)
                gated = mixed * sigma
                slope_ref[layer, s, rows, :] = (sigma + gated * (1.0 - sigma)).astype(BF16)
                cur[s] = (cur[s] + gated).astype(BF16).astype(F32)
        for s in range(count):
            out_ref[s, rows, :] = cur[s].astype(BF16)
        return carry

    lax.fori_loop(0, channels // 16, chunk, 0)


def power_of_two(e):
    up, down = F32(1.0), F32(1.0)
    size = jnp.abs(e)
    for bit in range(6):
        on = ((size >> bit) & 1) == 1
        up = up * jnp.where(on, F32(2.0 ** (1 << bit)), F32(1.0))
        down = down * jnp.where(on, F32(0.5 ** (1 << bit)), F32(1.0))
    return jnp.where(e >= 0, up, down), jnp.where(e >= 0, down, up)


def keyval_body(
    exp_ref, x_hbm, wkv_hbm, wq_hbm, send_hbm, trunk_hbm,
    x_ref, wkv_ref, wq_ref, send_ref, trunk_ref, sems,
):
    pairs = ((x_hbm, x_ref), (wkv_hbm, wkv_ref), (wq_hbm, wq_ref))
    reads = [pltpu.make_async_copy(a, b, sems.at[k]) for k, (a, b) in enumerate(pairs)]
    for copy in reads:
        copy.start()
    reads[0].wait()
    count, channels, _ = x_ref.shape
    for s in range(count):
        trunk_ref[:, s * channels : (s + 1) * channels] = x_ref[s].astype(F32).T.astype(BF16)
    writes = [pltpu.make_async_copy(trunk_ref, trunk_hbm, sems.at[3])]
    writes[0].start()
    factor, inverse = power_of_two(exp_ref[0])
    reads[1].wait()
    unscaled = nn(trunk_ref[...], wkv_ref[...]) * inverse
    codes = jnp.clip(unscaled, -CLIP_LEVEL, CLIP_LEVEL).astype(BF16).astype(F32)
    marked = jnp.where(
        jnp.abs(unscaled) < CLIP_LEVEL, codes, jnp.where(unscaled > 0.0, F32(512.0), F32(-512.0))
    )
    send_ref[:, :256] = (marked * factor).astype(BF16)
    reads[2].wait()
    send_ref[:, 256:] = nn(trunk_ref[...], wq_ref[...]).astype(BF16)
    for s in range(count):
        writes.append(pltpu.make_async_copy(send_ref, send_hbm.at[s], sems.at[4 + s]))
        writes[-1].start()
    for copy in writes:
        copy.wait()


def query_body(me_ref, *refs):
    columns, (pack_ref, cells_ref) = refs[:8], refs[8:]
    me = me_ref[0]
    x, y = me // 4, lax.rem(me, 4)
    count = cells_ref.shape[0]
    for k, ref in enumerate(columns):
        block = (x if k < 4 else 1 - x) * 4 + lax.rem(y + (0, 3, 1, 2)[k % 4], 4)
        cells_ref[block] = ref[512:, :]
        pack_ref[block, :512, :] = ref[:512, :]
    row = lax.broadcasted_iota(jnp.int32, (128, 512), 0)
    col = lax.broadcasted_iota(jnp.int32, (128, 512), 1)
    same_head = (row % 32) // 8 == col // 128
    target = (row % 8) - (col % 64)
    mirrored = jnp.zeros((64, 512), F32)
    for s in range(count):
        pick = jnp.where(same_head & (row < 96) & (target == -8 * s), F32(1.0), F32(0.0))
        mirrored += nn(cells_ref[s], pick.astype(BF16))
    lane = lax.broadcasted_iota(jnp.int32, (64, 128), 1)
    for h in range(4):
        one = mirrored[:, 128 * h : 128 * h + 128]
        other = jnp.concatenate([one, one], axis=0).T
        bias = 0.5 * (one + other[:64, :]) * F32(128.0**0.5)
        hi = bias.astype(BF16).astype(F32)
        both = jnp.where(lane < 64, hi, bias - hi).astype(BF16)
        for s in range(count):
            wide = both[8 * s : 8 * s + 8].astype(F32)
            wide = jnp.broadcast_to(wide[:, None, :], (8, POOL, 128)).reshape(128, 128)
            pack_ref[s, 512 + 128 * h : 640 + 128 * h, :] = wide.astype(BF16)
    for s in range(count):
        corner = cells_ref[s, 0:1, 127:128].astype(F32)
        pack_ref[s, 1024:, :] = jnp.broadcast_to(corner, (16, 128)).astype(BF16)


def attention_body(
    kv_ref, pack_ref, att_ref, gq_ref, out_ref,
    sum_ref, kx_ref, v_ref, kt_ref, vt_ref, qx_ref, s_ref, sl_ref, pb_ref, cb_ref,
):
    scale = F32(128.0**-0.5)
    count = kv_ref.shape[0]
    length = count * 128
    for s in range(count):
        rows = slice(128 * s, 128 * s + 128)
        level = pack_ref[s, 1024:1025, 0:1].astype(F32) * CLIP_LEVEL
        plain = jnp.clip(kv_ref[s, :, :256].astype(F32), -level, level)
        kx_ref[rows, :128] = plain[:, :128].astype(BF16)
        v_ref[rows, :] = plain[:, 128:].astype(BF16)
        kt_ref[:, rows] = plain[:, :128].T.astype(BF16)
        vt_ref[:, rows] = plain[:, 128:].T.astype(BF16)
        for h in range(4):
            here = slice(128 * h, 128 * h + 128)
            qx_ref[s, here, :128] = kv_ref[s, :, 256 + 128 * h : 384 + 128 * h]
            qx_ref[s, here, 128:] = pack_ref[s, 512 + 128 * h : 640 + 128 * h, :]
    row = lax.broadcasted_iota(jnp.int32, (length, 128), 0)
    lane = lax.broadcasted_iota(jnp.int32, (length, 128), 1)
    kx_ref[:, 128:] = jnp.where(lane % 64 == row // POOL, F32(1.0), F32(0.0)).astype(BF16)
    sum_ref[...] = jnp.zeros_like(sum_ref)

    size = 256
    pieces = [slice(c * size, (c + 1) * size) for c in range(length // size)]
    fold = (size // 8, 8, 512)

    def scores(b, i):
        top = None
        for r in pieces:
            part = nt(kx_ref[r, :], qx_ref[i])
            s_ref[b, r, :] = part
            part = jnp.max(part.reshape(fold), axis=0)
            top = part if top is None else jnp.maximum(top, part)
        return jnp.max(top, axis=0, keepdims=True)

    def weigh(b, i, top):
        total = mean = jnp.zeros((8, 512), F32)
        for r in pieces:
            weights = jnp.exp2((s_ref[b, r, :] - top) * (scale * F32(1.4426950408889634)))
            slope = nt(v_ref[r, :], pack_ref[i, :512, :])
            s_ref[b, r, :] = weights
            sl_ref[b, r, :] = slope
            total += jnp.sum(weights.reshape(fold), axis=0)
            mean += jnp.sum((weights * slope).reshape(fold), axis=0)
        inverse = 1.0 / jnp.sum(total, axis=0, keepdims=True)
        return inverse, jnp.sum(mean, axis=0, keepdims=True) * inverse

    def products(b, i, inverse, mean):
        query, grad = qx_ref[i][:, :128], pack_ref[i, :512, :]
        for r in pieces:
            probs = s_ref[b, r, :] * inverse
            probs_b = probs.astype(BF16)
            centred_b = (probs * (sl_ref[b, r, :] - mean)).astype(BF16)
            pb_ref[b, r, :] = probs_b
            cb_ref[b, r, :] = centred_b
            sum_ref[r, :128] += nn(centred_b, query)
            sum_ref[r, 128:] += nn(probs_b, grad)
        attended = nn(vt_ref[...], pb_ref[b]).astype(BF16)
        grad_q = (nn(kt_ref[...], cb_ref[b]) * scale).astype(BF16)
        for h in range(4):
            here = slice(128 * h, 128 * h + 128)
            att_ref[i, here, :] = attended[:, here]
            gq_ref[i, here, :] = grad_q[:, here]

    def step(part, carry):
        start = part * RUN
        stats = weigh(0, start, scores(0, start))
        for d in range(RUN):
            last = d == RUN - 1
            top = None if last else scores((d + 1) % 2, start + d + 1)
            products(d % 2, start + d, *stats)
            if not last:
                stats = weigh((d + 1) % 2, start + d + 1, top)
        return carry

    lax.fori_loop(0, count // RUN, step, 0)
    side = lax.broadcasted_iota(jnp.int32, (128, 256), 1)
    for s in range(count):
        level = pack_ref[s, 1024:1025, 0:1].astype(F32) * CLIP_LEVEL
        inside = jnp.abs(kv_ref[s, :, :256].astype(F32)) <= level
        part = sum_ref[128 * s : 128 * s + 128, :]
        part = jnp.where(side < 128, part * scale, part)
        out_ref[s] = jnp.where(inside, part, 0.0).astype(BF16)


def output_body(me_ref, trunk_ref, att_ref, wout_ref, out_ref):
    me = me_ref[0]
    total = trunk_ref[...].astype(F32)
    for h in range(4):
        here = slice(128 * h, 128 * h + 128)
        total += nn(att_ref[me, here, :].astype(F32).T.astype(BF16), wout_ref[here, :])
    out_ref[...] = total.astype(BF16)


def back_body(
    dil_ref, me_ref, x_ref, att_ref, gq_ref, gkv_ref, wq_ref, wkv_ref, taps_ref, slope_ref,
    out_ref, g_ref, turn_ref,
):
    offset = take_taps(me_ref[0], taps_ref, turn_ref)
    count, channels, _ = g_ref.shape
    mine = pl.ds(pl.multiple_of(me_ref[0] * channels, 16), channels)
    my_wq, my_wkv = wq_ref[mine, :], wkv_ref[mine, :]
    grad_out = jnp.zeros((channels, 512), F32)
    for s in range(count):
        turned = x_ref[s, channels:, :]
        g_ref[s] = turned.astype(F32) + nn(my_wq, gq_ref[s]) + nt(my_wkv, gkv_ref[s])
        grad_out += nt(turned, att_ref[s])
    half = channels // 2
    for s in range(count):
        cols = grad_out[:, 64 * s : 64 * s + 64]
        out_ref[s, channels:, :] = jnp.concatenate([cols[:half], cols[half:]], axis=1).astype(BF16)

    def chunk(c, carry):
        rows = pl.ds(pl.multiple_of(c * 16, 16), 16)
        flow = [g_ref[s, rows, :] for s in range(count)]
        tap = turn_ref[pl.ds(pl.multiple_of(offset + c * 16, 16), 16), :]
        for layer in (1, 0):
            t0, t1, t2 = (tap[:, 8 * layer + k : 8 * layer + k + 1] for k in range(3))
            pushed = [
                (flow[s] * slope_ref[layer, s, rows, :].astype(F32)).astype(BF16).astype(F32)
                for s in range(count)
            ]
            before, after = shifts(pushed, dil_ref[layer])
            flow = [
                flow[s] + t0 * after[s] + t1 * pushed[s] + t2 * before[s] for s in range(count)
            ]
        for s in range(count):
            out_ref[s, rows, :] = flow[s].astype(BF16)
        return carry

    lax.fori_loop(0, channels // 16, chunk, 0)


def weights_body(x_ref, gq_ref, gkv_ref, gq_out_ref, gkv_out_ref):
    count, channels, _ = x_ref.shape
    first = jnp.zeros(gq_out_ref.shape, F32)
    second = jnp.zeros(gkv_out_ref.shape, F32)
    for s in range(count):
        first += nt(x_ref[s], gq_ref[s])
        second += nn(x_ref[s], gkv_ref[s])
    gq_out_ref[...] = first.astype(BF16)
    gkv_out_ref[...] = second.astype(BF16)


def last_body(x_ref, grad_ref, gout_ref):
    count, wide, _ = x_ref.shape
    channels = grad_ref.shape[1] // count
    half = wide - channels
    for s in range(count):
        grad_ref[:, s * channels : (s + 1) * channels] = (
            x_ref[s, :channels, :].astype(F32).T.astype(BF16)
        )
        turned = x_ref[s, channels:, :].astype(F32).T.astype(BF16)
        gout_ref[:, s * channels : s * channels + half] = turned[:64]
        gout_ref[:, s * channels + half : (s + 1) * channels] = turned[64:]


def local(tokens, dilations, taps, w_query, w_keyval, w_out, exponents, pair, w_bias, cotangent):
    count = lax.axis_size("seq")
    me = lax.axis_index("seq")
    rows, width = tokens.shape
    ch = width // count
    length = rows * count
    place = me.astype(jnp.int32).reshape(1)
    blocks = (count, ch, rows)

    turned_shape = (count, 2 * ch, rows)
    (first,) = call(
        flip_body,
        [(turned_shape, BF16)],
        "flip",
        0,
        4 * rows * width,
        scratch=[
            pltpu.VMEM((rows, width), BF16),
            pltpu.VMEM((rows, width), BF16),
            pltpu.VMEM(turned_shape, BF16),
            pltpu.SemaphoreType.DMA((count + 2,)),
        ],
        limit=63,
        space=ANY,
    )(tokens, cotangent)
    turned = exchange(first)
    (grad_attn,) = call(
        early_body, [((576, 128), BF16)], "early", 2 * rows * width * 512, 4 * MIB
    )(exponents, cotangent, w_out, pair, w_bias.T)
    my_taps = jnp.transpose(taps, (1, 0, 2))
    turn = pltpu.VMEM((256, 16), F32)
    across = [(i, (i + 4) % 8) for i in range(8)]
    around = {o: [(i, i // 4 * 4 + (i + o) % 4) for i in range(8)] for o in (1, 2, 3)}
    columns = [grad_attn] + [lax.ppermute(grad_attn, "seq", around[o]) for o in (1, 3, 2)]

    other = [lax.ppermute(grad_attn, "seq", across)]

    trunk_turned, slopes = call(
        conv_body,
        [(blocks, BF16), ((2, *blocks), BF16)],
        "conv",
        100 * length * ch,
        4 * MIB,
        scratch=[turn],
        limit=CONV_LIMIT,
    )(dilations, place, after(turned, grad_attn), my_taps)
    back = exchange(after(trunk_turned, *columns, *other))
    other += [lax.ppermute(c, "seq", across) for c in columns[1:3]]
    other += [lax.ppermute(other[0], "seq", around[2])]

    keyval, trunk = call(
        keyval_body,
        [((count, rows, 768), BF16), ((rows, width), BF16)],
        "keyval",
        2 * rows * width * 768,
        2 * MIB,
        scratch=[
            pltpu.VMEM(blocks, BF16),
            pltpu.VMEM((width, 256), BF16),
            pltpu.VMEM((width, 512), BF16),
            pltpu.VMEM((rows, 768), BF16),
            pltpu.VMEM((rows, width), BF16),
            pltpu.SemaphoreType.DMA((4 + count,)),
        ],
        limit=63,
        space=ANY,
    )(exponents, back, w_keyval, w_query)
    keyval = exchange(after(keyval, *other))
    columns = columns + other
    (pack,) = call(
        query_body,
        [((count, 1040, 128), BF16)],
        "query",
        2 * rows * width * 512,
        3 * MIB,
        scratch=[pltpu.VMEM((count, 64, 128), BF16)],
    )(place, *columns)

    heads = (count, 512, 128)
    attended, grad_q, grad_kv = call(
        attention_body,
        [(heads, BF16), (heads, BF16), ((count, rows, 256), BF16)],
        "attention",
        12 * length * length * 512,
        8 * MIB,
        scratch=[
            pltpu.VMEM((length, 256), F32),
            pltpu.VMEM((length, 256), BF16),
            pltpu.VMEM((length, 128), BF16),
            pltpu.VMEM((128, length), BF16),
            pltpu.VMEM((128, length), BF16),
            pltpu.VMEM((count, 512, 256), BF16),
            pltpu.VMEM((2, length, 512), F32),
            pltpu.VMEM((2, length, 512), F32),
            pltpu.VMEM((2, length, 512), BF16),
            pltpu.VMEM((2, length, 512), BF16),
        ],
        limit=32,
    )(keyval, pack)

    (final,) = call(
        back_body,
        [((count, ch + ch // 2, rows), BF16)],
        "back",
        2 * length * ch * 1280,
        8 * MIB,
        scratch=[pltpu.VMEM(blocks, F32), turn],
    )(dilations, place, turned, attended, grad_q, grad_kv, w_query, w_keyval, my_taps, slopes)
    final = exchange(final)
    grad_query, grad_keyval = call(
        weights_body,
        [((ch, 512), BF16), ((ch, 256), BF16)],
        "weights",
        2 * length * ch * 768,
        4 * MIB,
    )(trunk_turned, grad_q, grad_kv)
    (output,) = call(output_body, [((rows, width), BF16)], "output", 2 * rows * width * 512, 3 * MIB)(
        place, trunk, attended, w_out
    )
    grad_tokens, grad_out = call(
        last_body, [((rows, width), BF16), ((64, width), BF16)], "last", 0, 2 * MIB
    )(final)
    return output, grad_tokens, grad_query, grad_keyval, grad_out


def solution(mesh):
    both = P(("dp", "seq"))
    in_specs = (both, P(), P(), P(), P(), P(), both, both, P(), both)
    return jax.shard_map(
        local, mesh=mesh, in_specs=in_specs, out_specs=(both,) * 5, check_vma=False
    )
```

```python
import jax
import jax.numpy as jnp
from jax import lax
from jax.experimental import pallas as pl
from jax.experimental.pallas import tpu as pltpu
from jax.sharding import PartitionSpec as P

POOL = 16
CLIP_LEVEL = 448.0
RUN = 8
CONV_LIMIT = 63
F32 = jnp.float32
BF16 = jnp.bfloat16
MIB = 1 << 20
VMEM = pl.BlockSpec(memory_space=pltpu.VMEM)
SMEM = pl.BlockSpec(memory_space=pltpu.SMEM)
ANY = pl.BlockSpec(memory_space=pl.ANY)


def nn(a, b):
    return jnp.dot(a, b, preferred_element_type=F32)


def nt(a, b):
    return lax.dot_general(a, b, (((1,), (1,)), ((), ())), preferred_element_type=F32)


def call(body, outs, name, flops=0, nbytes=0, scratch=(), limit=16, space=VMEM):
    def run(*args):
        return pl.pallas_call(
            body,
            out_shape=[jax.ShapeDtypeStruct(s, d) for s, d in outs],
            in_specs=[SMEM if a.dtype == jnp.int32 else space for a in args],
            out_specs=[space] * len(outs),
            scratch_shapes=list(scratch),
            compiler_params=pltpu.CompilerParams(vmem_limit_bytes=limit * MIB),
            cost_estimate=pl.CostEstimate(flops=flops, bytes_accessed=nbytes, transcendentals=0),
            name=name,
        )(*args)

    return run


def exchange(x):
    return lax.all_to_all(x, "seq", split_axis=0, concat_axis=0, tiled=True)


def after(x, *others):
    return lax.optimization_barrier((x, *others))[0]


def flip_body(tok_hbm, cot_hbm, out_hbm, tok_ref, cot_ref, out_ref, sems):
    n, rows, _ = out_ref.shape
    half = rows // 2
    reads = [
        pltpu.make_async_copy(tok_hbm, tok_ref, sems.at[n]),
        pltpu.make_async_copy(cot_hbm, cot_ref, sems.at[n + 1]),
    ]
    for copy in reads:
        copy.start()
    reads[0].wait()
    for r in range(n):
        out_ref[r, :half, :] = tok_ref[:, r * half : (r + 1) * half].astype(F32).T.astype(BF16)
    reads[1].wait()
    writes = []
    for r in range(n):
        out_ref[r, half:, :] = cot_ref[:, r * half : (r + 1) * half].astype(F32).T.astype(BF16)
        writes.append(pltpu.make_async_copy(out_ref.at[r], out_hbm.at[r], sems.at[r]))
        writes[r].start()
    for copy in writes:
        copy.wait()


def split3(x):
    hi = x.astype(BF16)
    rest = x - hi.astype(F32)
    mid = rest.astype(BF16)
    lo = (rest - mid.astype(F32)).astype(BF16)
    return hi, mid, lo


def take_taps(me, taps_ref, turn_ref):
    begin = me * 192
    window = begin // 128 * 128
    for k in range(3):
        part = taps_ref[k, :, pl.ds(pl.multiple_of(window, 128), 256)]
        for layer in range(2):
            turn_ref[:, 8 * layer + k : 8 * layer + k + 1] = part[layer : layer + 1, :].T
    return begin - window


def early_body(exp_ref, cot_ref, wout_ref, pair_ref, wb_ref, out_ref):
    weights = jnp.concatenate([wb_ref[...], wb_ref[...]], axis=0).T
    lane = lax.broadcasted_iota(jnp.int32, (128, 128), 1)
    head = (lane % 32) // 8
    wide = jnp.zeros((128, 128), F32)
    for h in range(4):
        wide = jnp.where(head == h, weights[:, h : h + 1], wide)
    pieces = split3(wide)
    cells = jnp.zeros((64, 128), F32)
    for j in range(8):
        pick = lane % 8 == j
        for piece in pieces:
            cells += nn(pair_ref[j], jnp.where(pick, piece.astype(F32), 0.0).astype(BF16))
    hi, mid, lo = (piece.astype(F32) for piece in split3(cells))
    group = lax.broadcasted_iota(jnp.int32, (64, 128), 1) // 32
    factor, _ = power_of_two(exp_ref[0])
    packed = jnp.where(group == 0, hi, jnp.where(group == 1, mid, jnp.where(group == 2, lo, factor)))
    out_ref[512:, :] = packed.astype(BF16)
    grad = nt(cot_ref[...], wout_ref[...]).astype(BF16)
    for h in range(4):
        out_ref[128 * h : 128 * h + 128, :] = grad[:, 128 * h : 128 * h + 128]


def sigmoid(v):
    return 0.5 * jnp.tanh(0.5 * v) + 0.5


def shifts(blocks, d):
    lane = lax.broadcasted_iota(jnp.int32, blocks[0].shape, 1)
    turn = lax.rem(d, 128)
    back = 128 - d
    rolled = [pltpu.roll(b, turn, 1) for b in blocks]
    other = [pltpu.roll(b, back, 1) for b in blocks]
    zero = jnp.zeros_like(blocks[0])
    count = len(blocks)
    before = [
        jnp.where(lane < d, rolled[s - 1] if s else zero, rolled[s]) for s in range(count)
    ]
    after = [
        jnp.where(lane >= back, other[s + 1] if s + 1 < count else zero, other[s])
        for s in range(count)
    ]
    return before, after


def conv_body(dil_ref, me_ref, x_ref, taps_ref, out_ref, slope_ref, turn_ref):
    offset = take_taps(me_ref[0], taps_ref, turn_ref)
    count, channels, _ = out_ref.shape

    def chunk(c, carry):
        rows = pl.ds(pl.multiple_of(c * 16, 16), 16)
        cur = [x_ref[s, rows, :].astype(F32) for s in range(count)]
        tap = turn_ref[pl.ds(pl.multiple_of(offset + c * 16, 16), 16), :]
        for layer in range(2):
            t0, t1, t2 = (tap[:, 8 * layer + k : 8 * layer + k + 1] for k in range(3))
            before, after = shifts(cur, dil_ref[layer])
            for s in range(count):
                mixed = t0 * before[s] + t1 * cur[s] + t2 * after[s]
                sigma = sigmoid(mixed)
                gated = mixed * sigma
                slope_ref[layer, s, rows, :] = (sigma + gated * (1.0 - sigma)).astype(BF16)
                cur[s] = (cur[s] + gated).astype(BF16).astype(F32)
        for s in range(count):
            out_ref[s, rows, :] = cur[s].astype(BF16)
        return carry

    lax.fori_loop(0, channels // 16, chunk, 0)


def power_of_two(e):
    up, down = F32(1.0), F32(1.0)
    size = jnp.abs(e)
    for bit in range(6):
        on = ((size >> bit) & 1) == 1
        up = up * jnp.where(on, F32(2.0 ** (1 << bit)), F32(1.0))
        down = down * jnp.where(on, F32(0.5 ** (1 << bit)), F32(1.0))
    return jnp.where(e >= 0, up, down), jnp.where(e >= 0, down, up)


def keyval_body(
    exp_ref, x_hbm, wkv_hbm, wq_hbm, send_hbm, trunk_hbm,
    x_ref, wkv_ref, wq_ref, send_ref, trunk_ref, sems,
):
    pairs = ((x_hbm, x_ref), (wkv_hbm, wkv_ref), (wq_hbm, wq_ref))
    reads = [pltpu.make_async_copy(a, b, sems.at[k]) for k, (a, b) in enumerate(pairs)]
    for copy in reads:
        copy.start()
    reads[0].wait()
    count, channels, _ = x_ref.shape
    for s in range(count):
        trunk_ref[:, s * channels : (s + 1) * channels] = x_ref[s].astype(F32).T.astype(BF16)
    writes = [pltpu.make_async_copy(trunk_ref, trunk_hbm, sems.at[3])]
    writes[0].start()
    factor, inverse = power_of_two(exp_ref[0])
    reads[1].wait()
    unscaled = nn(trunk_ref[...], wkv_ref[...]) * inverse
    codes = jnp.clip(unscaled, -CLIP_LEVEL, CLIP_LEVEL).astype(BF16).astype(F32)
    marked = jnp.where(
        jnp.abs(unscaled) < CLIP_LEVEL, codes, jnp.where(unscaled > 0.0, F32(512.0), F32(-512.0))
    )
    send_ref[:, :256] = (marked * factor).astype(BF16)
    reads[2].wait()
    send_ref[:, 256:] = nn(trunk_ref[...], wq_ref[...]).astype(BF16)
    for s in range(count):
        writes.append(pltpu.make_async_copy(send_ref, send_hbm.at[s], sems.at[4 + s]))
        writes[-1].start()
    for copy in writes:
        copy.wait()


def query_body(me_ref, *refs):
    columns, (pack_ref, cells_ref) = refs[:8], refs[8:]
    me = me_ref[0]
    x, y = me // 4, lax.rem(me, 4)
    count = cells_ref.shape[0]
    for k, ref in enumerate(columns):
        block = (x if k < 4 else 1 - x) * 4 + lax.rem(y + (0, 3, 1, 2)[k % 4], 4)
        cells_ref[block] = ref[512:, :]
        pack_ref[block, :512, :] = ref[:512, :]
    row = lax.broadcasted_iota(jnp.int32, (128, 512), 0)
    col = lax.broadcasted_iota(jnp.int32, (128, 512), 1)
    same_head = (row % 32) // 8 == col // 128
    target = (row % 8) - (col % 64)
    mirrored = jnp.zeros((64, 512), F32)
    for s in range(count):
        pick = jnp.where(same_head & (row < 96) & (target == -8 * s), F32(1.0), F32(0.0))
        mirrored += nn(cells_ref[s], pick.astype(BF16))
    lane = lax.broadcasted_iota(jnp.int32, (64, 128), 1)
    both = []
    for h in range(4):
        one = mirrored[:, 128 * h : 128 * h + 128]
        other = jnp.concatenate([one, one], axis=0).T
        bias = 0.5 * (one + other[:64, :]) * F32(128.0**0.5)
        hi = bias.astype(BF16).astype(F32)
        both.append(jnp.where(lane < 64, hi, bias - hi))
    for s in range(count):
        rows = jnp.concatenate([b[8 * s : 8 * s + 8] for b in both], axis=0)
        pack_ref[s, 512:544, :] = rows.astype(BF16)
    for s in range(count):
        corner = cells_ref[s, 0:1, 127:128].astype(F32)
        pack_ref[s, 544:, :] = jnp.broadcast_to(corner, (16, 128)).astype(BF16)


def attention_body(
    kv_ref, pack_ref, att_ref, gq_ref,
    sum_ref, kx_ref, v_ref, kt_ref, vt_ref, qx_ref, s_ref, sl_ref, pb_ref, cb_ref,
):
    scale = F32(128.0**-0.5)
    count = kv_ref.shape[0]
    length = count * 128
    for s in range(count):
        rows = slice(128 * s, 128 * s + 128)
        level = pack_ref[s, 544:560, :][0:1, 0:1].astype(F32) * CLIP_LEVEL
        plain = jnp.clip(kv_ref[s, :, :256].astype(F32), -level, level)
        kx_ref[rows, :128] = plain[:, :128].astype(BF16)
        v_ref[rows, :] = plain[:, 128:].astype(BF16)
        kt_ref[:, rows] = plain[:, :128].T.astype(BF16)
        vt_ref[:, rows] = plain[:, 128:].T.astype(BF16)
        bias = pack_ref[s, 512:544, :].astype(F32)
        for h in range(4):
            here = slice(128 * h, 128 * h + 128)
            qx_ref[s, here, :128] = kv_ref[s, :, 256 + 128 * h : 384 + 128 * h]
            wide = jnp.broadcast_to(bias[8 * h : 8 * h + 8][:, None, :], (8, POOL, 128))
            qx_ref[s, here, 128:] = wide.reshape(128, 128).astype(BF16)
    row = lax.broadcasted_iota(jnp.int32, (length, 128), 0)
    lane = lax.broadcasted_iota(jnp.int32, (length, 128), 1)
    kx_ref[:, 128:] = jnp.where(lane % 64 == row // POOL, F32(1.0), F32(0.0)).astype(BF16)
    sum_ref[...] = jnp.zeros_like(sum_ref)

    size = 256
    pieces = [slice(c * size, (c + 1) * size) for c in range(length // size)]
    fold = (size // 8, 8, 512)

    def scores(b, i):
        top = None
        for r in pieces:
            part = nt(kx_ref[r, :], qx_ref[i])
            s_ref[b, r, :] = part
            part = jnp.max(part.reshape(fold), axis=0)
            top = part if top is None else jnp.maximum(top, part)
        return jnp.max(top, axis=0, keepdims=True)

    def weigh(b, i, top):
        total = mean = jnp.zeros((8, 512), F32)
        for r in pieces:
            weights = jnp.exp2((s_ref[b, r, :] - top) * (scale * F32(1.4426950408889634)))
            slope = nt(v_ref[r, :], pack_ref[i, :512, :])
            s_ref[b, r, :] = weights
            sl_ref[b, r, :] = slope
            total += jnp.sum(weights.reshape(fold), axis=0)
            mean += jnp.sum((weights * slope).reshape(fold), axis=0)
        inverse = 1.0 / jnp.sum(total, axis=0, keepdims=True)
        return inverse, jnp.sum(mean, axis=0, keepdims=True) * inverse

    def products(b, i, inverse, mean):
        query, grad = qx_ref[i][:, :128], pack_ref[i, :512, :]
        for r in pieces:
            probs = s_ref[b, r, :] * inverse
            probs_b = probs.astype(BF16)
            centred_b = (probs * (sl_ref[b, r, :] - mean)).astype(BF16)
            pb_ref[b, r, :] = probs_b
            cb_ref[b, r, :] = centred_b
            sum_ref[r, :128] += nn(centred_b, query)
            sum_ref[r, 128:] += nn(probs_b, grad)
        attended = nn(vt_ref[...], pb_ref[b]).astype(BF16)
        grad_q = (nn(kt_ref[...], cb_ref[b]) * scale).astype(BF16)
        for h in range(4):
            here = slice(128 * h, 128 * h + 128)
            att_ref[i, here, :] = attended[:, here]
            gq_ref[i, here, :] = grad_q[:, here]

    def step(part, carry):
        start = part * RUN
        stats = weigh(0, start, scores(0, start))
        for d in range(RUN):
            last = d == RUN - 1
            top = None if last else scores((d + 1) % 2, start + d + 1)
            products(d % 2, start + d, *stats)
            if not last:
                stats = weigh((d + 1) % 2, start + d + 1, top)
        return carry

    lax.fori_loop(0, count // RUN, step, 0)
    side = lax.broadcasted_iota(jnp.int32, (128, 256), 1)
    for s in range(count):
        level = pack_ref[s, 544:560, :][0:1, 0:1].astype(F32) * CLIP_LEVEL
        inside = jnp.abs(kv_ref[s, :, :256].astype(F32)) <= level
        part = sum_ref[128 * s : 128 * s + 128, :]
        part = jnp.where(side < 128, part * scale, part)
        part = jnp.where(inside, part, 0.0).astype(BF16)
        gq_ref[s, 512:640, :] = part[:, :128]
        gq_ref[s, 640:, :] = part[:, 128:]


def output_body(me_ref, trunk_ref, att_ref, wout_ref, out_ref):
    me = me_ref[0]
    total = trunk_ref[...].astype(F32)
    for h in range(4):
        here = slice(128 * h, 128 * h + 128)
        total += nn(att_ref[me, here, :].astype(F32).T.astype(BF16), wout_ref[here, :])
    out_ref[...] = total.astype(BF16)


def back_body(
    dil_ref, me_ref, x_ref, att_ref, gq_ref, wq_ref, wkv_ref, taps_ref, slope_ref,
    out_ref, g_ref, turn_ref,
):
    offset = take_taps(me_ref[0], taps_ref, turn_ref)
    count, channels, _ = g_ref.shape
    mine = pl.ds(pl.multiple_of(me_ref[0] * channels, 16), channels)
    my_wq, my_wkv = wq_ref[mine, :], wkv_ref[mine, :]
    grad_out = jnp.zeros((channels, 512), F32)
    for s in range(count):
        turned = x_ref[s, channels:, :]
        g_ref[s] = turned.astype(F32) + nn(my_wq, gq_ref[s, :512, :])
        g_ref[s] += nt(my_wkv[:, :128], gq_ref[s, 512:640, :]) + nt(my_wkv[:, 128:], gq_ref[s, 640:, :])
        grad_out += nt(turned, att_ref[s])
    half = channels // 2
    for s in range(count):
        cols = grad_out[:, 64 * s : 64 * s + 64]
        out_ref[s, channels:, :] = jnp.concatenate([cols[:half], cols[half:]], axis=1).astype(BF16)

    def chunk(c, carry):
        rows = pl.ds(pl.multiple_of(c * 16, 16), 16)
        flow = [g_ref[s, rows, :] for s in range(count)]
        tap = turn_ref[pl.ds(pl.multiple_of(offset + c * 16, 16), 16), :]
        for layer in (1, 0):
            t0, t1, t2 = (tap[:, 8 * layer + k : 8 * layer + k + 1] for k in range(3))
            pushed = [
                (flow[s] * slope_ref[layer, s, rows, :].astype(F32)).astype(BF16).astype(F32)
                for s in range(count)
            ]
            before, after = shifts(pushed, dil_ref[layer])
            flow = [
                flow[s] + t0 * after[s] + t1 * pushed[s] + t2 * before[s] for s in range(count)
            ]
        for s in range(count):
            out_ref[s, rows, :] = flow[s].astype(BF16)
        return carry

    lax.fori_loop(0, channels // 16, chunk, 0)


def weights_body(x_ref, gq_ref, gq_out_ref, gkv_out_ref):
    count, channels, _ = x_ref.shape
    first = jnp.zeros(gq_out_ref.shape, F32)
    second = [jnp.zeros((channels, 128), F32) for _ in range(2)]
    for s in range(count):
        first += nt(x_ref[s], gq_ref[s, :512, :])
        second[0] += nn(x_ref[s], gq_ref[s, 512:640, :])
        second[1] += nn(x_ref[s], gq_ref[s, 640:, :])
    gq_out_ref[...] = first.astype(BF16)
    gkv_out_ref[:, :128] = second[0].astype(BF16)
    gkv_out_ref[:, 128:] = second[1].astype(BF16)


def last_body(x_ref, grad_ref, gout_ref):
    count, wide, _ = x_ref.shape
    channels = grad_ref.shape[1] // count
    half = wide - channels
    for s in range(count):
        grad_ref[:, s * channels : (s + 1) * channels] = (
            x_ref[s, :channels, :].astype(F32).T.astype(BF16)
        )
        turned = x_ref[s, channels:, :].astype(F32).T.astype(BF16)
        gout_ref[:, s * channels : s * channels + half] = turned[:64]
        gout_ref[:, s * channels + half : (s + 1) * channels] = turned[64:]


def local(tokens, dilations, taps, w_query, w_keyval, w_out, exponents, pair, w_bias, cotangent):
    count = lax.axis_size("seq")
    me = lax.axis_index("seq")
    rows, width = tokens.shape
    ch = width // count
    length = rows * count
    place = me.astype(jnp.int32).reshape(1)
    blocks = (count, ch, rows)

    turned_shape = (count, 2 * ch, rows)
    (first,) = call(
        flip_body,
        [(turned_shape, BF16)],
        "flip",
        0,
        4 * rows * width,
        scratch=[
            pltpu.VMEM((rows, width), BF16),
            pltpu.VMEM((rows, width), BF16),
            pltpu.VMEM(turned_shape, BF16),
            pltpu.SemaphoreType.DMA((count + 2,)),
        ],
        limit=63,
        space=ANY,
    )(tokens, cotangent)
    turned = exchange(first)
    (grad_attn,) = call(
        early_body, [((576, 128), BF16)], "early", 2 * rows * width * 512, 4 * MIB
    )(exponents, cotangent, w_out, pair, w_bias.T)
    my_taps = jnp.transpose(taps, (1, 0, 2))
    turn = pltpu.VMEM((256, 16), F32)
    across = [(i, (i + 4) % 8) for i in range(8)]
    around = {o: [(i, i // 4 * 4 + (i + o) % 4) for i in range(8)] for o in (1, 2, 3)}
    columns = [grad_attn] + [lax.ppermute(grad_attn, "seq", around[o]) for o in (1, 3, 2)]

    other = [lax.ppermute(grad_attn, "seq", across)]

    trunk_turned, slopes = call(
        conv_body,
        [(blocks, BF16), ((2, *blocks), BF16)],
        "conv",
        100 * length * ch,
        4 * MIB,
        scratch=[turn],
        limit=CONV_LIMIT,
    )(dilations, place, after(turned, grad_attn), my_taps)
    back = exchange(after(trunk_turned, *columns, *other))
    other += [lax.ppermute(c, "seq", across) for c in columns[1:3]]
    other += [lax.ppermute(other[0], "seq", around[2])]

    keyval, trunk = call(
        keyval_body,
        [((count, rows, 768), BF16), ((rows, width), BF16)],
        "keyval",
        2 * rows * width * 768,
        2 * MIB,
        scratch=[
            pltpu.VMEM(blocks, BF16),
            pltpu.VMEM((width, 256), BF16),
            pltpu.VMEM((width, 512), BF16),
            pltpu.VMEM((rows, 768), BF16),
            pltpu.VMEM((rows, width), BF16),
            pltpu.SemaphoreType.DMA((4 + count,)),
        ],
        limit=63,
        space=ANY,
    )(exponents, back, w_keyval, w_query)
    keyval = exchange(after(keyval, *other))
    columns = columns + other
    (pack,) = call(
        query_body,
        [((count, 560, 128), BF16)],
        "query",
        2 * rows * width * 512,
        3 * MIB,
        scratch=[pltpu.VMEM((count, 64, 128), BF16)],
    )(place, *columns)

    heads = (count, 512, 128)
    attended, grad_q = call(
        attention_body,
        [(heads, BF16), ((count, 768, 128), BF16)],
        "attention",
        12 * length * length * 512,
        8 * MIB,
        scratch=[
            pltpu.VMEM((length, 256), F32),
            pltpu.VMEM((length, 256), BF16),
            pltpu.VMEM((length, 128), BF16),
            pltpu.VMEM((128, length), BF16),
            pltpu.VMEM((128, length), BF16),
            pltpu.VMEM((count, 512, 256), BF16),
            pltpu.VMEM((2, length, 512), F32),
            pltpu.VMEM((2, length, 512), F32),
            pltpu.VMEM((2, length, 512), BF16),
            pltpu.VMEM((2, length, 512), BF16),
        ],
        limit=32,
    )(keyval, pack)

    (final,) = call(
        back_body,
        [((count, ch + ch // 2, rows), BF16)],
        "back",
        2 * length * ch * 1280,
        8 * MIB,
        scratch=[pltpu.VMEM(blocks, F32), turn],
    )(dilations, place, turned, attended, grad_q, w_query, w_keyval, my_taps, slopes)
    final = exchange(final)
    grad_query, grad_keyval = call(
        weights_body,
        [((ch, 512), BF16), ((ch, 256), BF16)],
        "weights",
        2 * length * ch * 768,
        4 * MIB,
    )(trunk_turned, grad_q)
    (output,) = call(output_body, [((rows, width), BF16)], "output", 2 * rows * width * 512, 3 * MIB)(
        place, trunk, attended, w_out
    )
    grad_tokens, grad_out = call(
        last_body, [((rows, width), BF16), ((64, width), BF16)], "last", 0, 2 * MIB
    )(final)
    return output, grad_tokens, grad_query, grad_keyval, grad_out


def solution(mesh):
    both = P(("dp", "seq"))
    in_specs = (both, P(), P(), P(), P(), P(), both, both, P(), both)
    return jax.shard_map(
        local, mesh=mesh, in_specs=in_specs, out_specs=(both,) * 5, check_vma=False
    )
```
